32 devices in a mesh: row: 8 (over z, core), col: 4 (over y, x).
Axes of the slice: x: 2, y: 2, z: 4, core: 2. Of those that a mesh axis runs over, the one named last changes fastest.
Arguments:
- train_points: float32 [64, 2048], P(None, ('row', 'col')), may hold values from -6 to 6
- cand_points: float32 [64, 2048], P(None, ('row', 'col')), may hold values from -6 to 6
- inv_length: float32 [64], replicated, may hold values from 0.04 to 0.7
- noise: float32 [2048], P(('row', 'col')), may hold values from 0.5 to 4
- targets: float32 [16, 2048], P(None, ('row', 'col')), may hold values from -15 to 15
Outputs:
- solution: float32 [16, 2048], P(None, ('row', 'col'))
- post_mean: float32 [16, 2048], P(None, ('row', 'col'))
The draws below stay inside these ranges and needn't reach their ends.
All inputs are finite; a program needn't handle non-finite values.
Results may differ from the reference program's by a relative error of at most 0.0047.
Values may be sent and summed in bfloat16 or wider, within the bound.
A program may use at most 64 MiB of HBM per device.

```python
import math
import jax
import jax.numpy as jnp
from jax import lax

D = 64
RHS = 16
ITERS = 2
TRAIN = 2048
CAND = 2048


def draw_targets(key, part):
    first, second = jax.random.split(key, 2)
    position = jnp.arange(TRAIN, dtype=jnp.float32) / max(TRAIN - 1, 1)
    column_scale = jnp.exp(jax.random.uniform(second, (TRAIN,), jnp.float32, 0.0, math.log(10.0))) * (0.5 + position) * 0.25
    base = jnp.clip(jax.random.normal(first, (RHS, TRAIN), jnp.float32), -4.0, 4.0)
    return base * column_scale[None, :]


def steps_of(own_key, dims, shards, least, high):
    def one(axis_at, blocks):
        draws = jax.random.uniform(jax.random.fold_in(jax.random.fold_in(own_key, 6), axis_at), (blocks,), jnp.float32, least / len(shards), high / len(shards))
        return jnp.repeat(jnp.exp(draws), dims[axis_at] // blocks).reshape((-1,) + (1,) * (len(dims) - axis_at - 1))

    loudness = one(*shards[0])
    for cut in shards[1:]:
        loudness = loudness * one(*cut)
    return loudness


def gaussian(own_key, extent, deviation, reach, pieces=(), held_as=jnp.bfloat16):
    gain = steps_of(own_key, extent, pieces, -0.22, 0.18) if pieces else 1.0
    entries = jax.random.normal(own_key, extent, jnp.float32) * deviation * gain
    return jnp.minimum(jnp.maximum(entries, -reach), reach).astype(held_as)


def setup_inputs(seed: int = 0) -> dict:
    key_list = jax.random.split(jax.random.key(seed), 6)
    train_points = gaussian(key_list[0], (D, TRAIN), 1.0, 6.0, ((1, 32),), jnp.float32)
    cand_points = gaussian(key_list[1], (D, CAND), 1.0, 6.0, ((1, 32),), jnp.float32)
    inv_length = jnp.clip(jnp.exp(jax.random.uniform(key_list[2], (D,), jnp.float32, math.log(0.04), math.log(0.7))), 0.04, 0.7)
    noise = jnp.clip(jnp.exp(math.log(4.0) - 2.0794415 * jax.random.uniform(key_list[3], (TRAIN,), jnp.float32) ** steps_of(key_list[3], (TRAIN,), ((0, 32),), -0.2, 0.2)), 0.5, 4.0)
    targets = draw_targets(jax.random.fold_in(key_list[5], 71), 0)
    return {"train_points": train_points, "cand_points": cand_points, "inv_length": inv_length, "noise": noise, "targets": targets}


root_five = math.sqrt(5.0)

def matern(left, left_norm, right, right_norm):
    inner = lax.dot_general(left, right, (((0,), (0,)), ((), ())), preferred_element_type=jnp.float32)
    dist_sq = jnp.maximum(left_norm[:, None] + right_norm[None, :] - 2.0 * inner, 0.0)
    radius = jnp.sqrt(dist_sq)
    return (1.0 + root_five * radius + 5.0 / 3.0 * dist_sq) * jnp.exp(-root_five * radius)

def kernel_apply(vector, points, norms, other, other_norms):
    size = points.shape[1]
    block = math.gcd(size, 512)

    def advance(total, index):
        offset = (index * block).astype(jnp.int32)
        sub_points = lax.dynamic_slice_in_dim(points, offset, block, 1)
        sub_norms = lax.dynamic_slice_in_dim(norms, offset, block, 0)
        sub_vector = lax.dynamic_slice_in_dim(vector, offset, block, 1)
        kernel_tile = matern(sub_points, sub_norms, other, other_norms)
        return (total + jnp.dot(sub_vector, kernel_tile, precision=lax.Precision.HIGHEST, preferred_element_type=jnp.float32), None)
    start_total = jnp.zeros((vector.shape[0], other.shape[1]), jnp.float32)
    total, _ = lax.scan(advance, start_total, jnp.arange(size // block, dtype=jnp.int32))
    return total

def reference(train_points, cand_points, inv_length, noise, targets):
    scaled_train = (train_points * inv_length[:, None]).astype(jnp.bfloat16)
    scaled_cand = (cand_points * inv_length[:, None]).astype(jnp.bfloat16)
    train_norms = lax.optimization_barrier(jnp.sum(jnp.square(scaled_train.astype(jnp.float32)), axis=0))
    cand_norms = lax.optimization_barrier(jnp.sum(jnp.square(scaled_cand.astype(jnp.float32)), axis=0))
    solution = jnp.zeros_like(targets)
    residual = targets
    direction = targets
    norm_now = lax.optimization_barrier(jnp.sum(residual * residual, axis=1))
    for iteration in range(ITERS):
        image = kernel_apply(direction, scaled_train, train_norms, scaled_train, train_norms) + noise[None, :] * direction
        alpha = norm_now / lax.optimization_barrier(jnp.sum(direction * image, axis=1))
        solution = solution + alpha[:, None] * direction
        residual = residual - alpha[:, None] * image
        norm_next = lax.optimization_barrier(jnp.sum(residual * residual, axis=1))
        direction = residual + (norm_next / norm_now)[:, None] * direction
        norm_now = norm_next
    post_mean = kernel_apply(solution, scaled_train, train_norms, scaled_cand, cand_norms)
    return (solution, post_mean)
```

```python
import functools
import math

import jax
import jax.numpy as jnp
from jax import lax
from jax.experimental import pallas as pl
from jax.experimental.pallas import tpu as pltpu
from jax.sharding import PartitionSpec as P

MESH = pl.DeviceIdType.MESH
root_five = math.sqrt(5.0)
F32 = jnp.float32
BF16 = jnp.bfloat16


def lanes_of(rows):
    return lax.broadcasted_iota(jnp.int32, (rows, 128), 1)


def rounded(value):
    return value.astype(BF16).astype(F32)


def halves(doubled):
    high = rounded(doubled)
    return jnp.where(lanes_of(doubled.shape[0]) < 64, high, doubled - high).astype(BF16)


def whole(block):
    value = block.astype(F32)
    return value + pltpu.roll(value, 64, 1)


def doubled(value):
    return jnp.where(lanes_of(value.shape[0]) < 64, value, pltpu.roll(value, 64, 1))


def point_forms(points):
    amount, dims = points.shape
    norm = jnp.sum(points * points, axis=1, keepdims=True)
    high = rounded(norm)
    middle = rounded(norm - high)
    low = rounded(norm - high - middle)
    lane = lanes_of(amount)
    padded = jnp.concatenate([points, jnp.zeros((amount, 128 - dims), F32)], axis=1)
    left, right = padded, -2.0 * padded
    for place, part in enumerate((high, middle, low)):
        left = jnp.where(lane == dims + place, part, left)
        left = jnp.where(lane == dims + 3 + place, 1.0, left)
        right = jnp.where(lane == dims + place, 1.0, right)
        right = jnp.where(lane == dims + 3 + place, part, right)
    return left.astype(BF16), right.astype(BF16)


def matern_split(left, right):
    dist = lax.dot_general(
        left, right, (((1,), (1,)), ((), ())), preferred_element_type=F32
    )
    dist = jnp.maximum(dist, 0.0)
    scaled = root_five * dist * lax.rsqrt(jnp.maximum(dist, 1e-30))
    kern = (1.0 + scaled + (5.0 / 3.0) * dist) * jnp.exp(-scaled)
    high = kern.astype(BF16)
    return high, (kern - high.astype(F32)).astype(BF16)


def apply_tile(block, high, low):
    return jnp.dot(
        jnp.concatenate([block, block], axis=1),
        jnp.concatenate([high, high, low, low], axis=0),
        preferred_element_type=F32,
    )


def column(value, lane_at):
    return jnp.sum(
        jnp.where(lanes_of(value.shape[0]) == lane_at, value, 0.0), axis=1, keepdims=True
    )


def kernel(
    rows, cols,
    train_ref, cand_ref, inv_ref, noise_ref, target_ref,
    solution_ref, mean_ref,
    ibuf, jbuf, cbuf, ktrain, kcand, psend, pbuf, vown, vrow, vcol, wsend, wbuf, sbuf,
    i_send, i_recv, j_send, j_recv, c_send, c_recv, p_send, p_recv,
    vr_send, vr_recv, vc_send, vc_recv, w_send, w_recv, s_send, s_recv,
):
    a = lax.axis_index("row")
    b = lax.axis_index("col")
    row_peers = [lax.rem(a + k, rows) for k in range(1, rows)]
    col_peers = [lax.rem(b + k, cols) for k in range(1, cols)]

    barrier = pltpu.get_barrier_semaphore()
    for p in row_peers:
        pl.semaphore_signal(barrier, inc=1, device_id=(p, b), device_id_type=MESH)
    for p in col_peers:
        pl.semaphore_signal(barrier, inc=1, device_id=(a, p), device_id_type=MESH)

    def to_row(src, buf, send, recv):
        return [
            pltpu.make_async_remote_copy(
                src_ref=src, dst_ref=buf.at[a], send_sem=send.at[p], recv_sem=recv.at[a],
                device_id=(p, b), device_id_type=MESH,
            )
            for p in row_peers
        ]

    def to_col(src, buf, send, recv):
        return [
            pltpu.make_async_remote_copy(
                src_ref=src(p), dst_ref=buf.at[b], send_sem=send.at[p], recv_sem=recv.at[b],
                device_id=(a, p), device_id_type=MESH,
            )
            for p in col_peers
        ]

    def arrived(buf, recv, p):
        pltpu.make_async_remote_copy(
            src_ref=buf.at[p], dst_ref=buf.at[p], send_sem=recv.at[p], recv_sem=recv.at[p],
            device_id=(a, b), device_id_type=MESH,
        ).wait_recv()

    lane = lanes_of(16)
    left_half = lane < 64

    points = jnp.concatenate([train_ref[...], cand_ref[...]], axis=1).T * inv_ref[...]
    left, right = point_forms(rounded(points))
    own_points = train_ref.shape[1]
    target = target_ref[...]
    target2 = jnp.concatenate([target, target], axis=1)
    target_block = halves(target2)
    noise = noise_ref[...]
    noise2 = jnp.concatenate([noise, noise], axis=1)
    ibuf[a, 0:64, :] = left[:own_points]
    ibuf[a, 64:80, :] = target_block
    jbuf[b, 0:64, :] = right[:own_points]
    jbuf[b, 64:80, :] = target_block
    cbuf[b] = right[own_points:]

    pl.semaphore_wait(barrier, rows + cols - 2)
    sent = to_row(ibuf.at[a], ibuf, i_send, i_recv)
    sent += to_col(lambda p: jbuf.at[b], jbuf, j_send, j_recv)
    sent += to_col(lambda p: cbuf.at[b], cbuf, c_send, c_recv)
    for copy in sent:
        copy.start()

    for p in col_peers:
        arrived(jbuf, j_recv, p)
    right_train = jbuf[:, 0:64, :].reshape(cols * 64, 128)
    partial = jnp.zeros((16, cols * 64), F32)
    for k in range(rows):
        p = a if k == 0 else row_peers[k - 1]
        if k:
            arrived(ibuf, i_recv, p)
        high, low = matern_split(ibuf[p, 0:64, :], right_train)
        ktrain[p, 0:64, :] = high
        ktrain[p, 64:128, :] = low
        partial += apply_tile(ibuf[p, 64:80, :], high, low)

    def over_columns(block_of):
        return [
            jnp.where(left_half, block_of(2 * h), block_of(2 * h + 1))
            for h in range(cols // 2)
        ]

    target_cols = over_columns(lambda s: whole(jbuf[s, 64:80, :]))

    def inner(wide, blocks):
        total = jnp.zeros((16, 128), F32)
        for h, block in enumerate(blocks):
            total += wide[:, 128 * h : 128 * h + 128] * block
        return jnp.sum(total, axis=1, keepdims=True)

    own_bb = jnp.sum(target * target, axis=1, keepdims=True)
    own_bnb = jnp.sum(noise * target * target, axis=1, keepdims=True)
    scalars = jnp.where(
        lane == 64, inner(partial, target_cols) + own_bnb, jnp.where(lane == 65, own_bb, 0.0)
    )
    for s in range(cols):
        piece = partial[:, 128 * (s // 2) : 128 * (s // 2) + 128]
        if s % 2:
            piece = pltpu.roll(piece, 64, 1)
        psend[s] = jnp.where(left_half, piece, scalars)
    copies = to_col(lambda p: psend.at[p], pbuf, p_send, p_recv)
    for copy in copies:
        copy.start()
    sent += copies

    for p in col_peers:
        arrived(cbuf, c_recv, p)
    right_cand = cbuf[...].reshape(cols * 64, 128)
    mean_b = jnp.zeros((16, cols * 64), F32)
    for k in range(rows):
        high, low = matern_split(ibuf[k, 0:64, :], right_cand)
        kcand[k, 0:64, :] = high
        kcand[k, 64:128, :] = low
        mean_b += apply_tile(ibuf[k, 64:80, :], high, low)

    image = psend[b]
    for p in col_peers:
        arrived(pbuf, p_recv, p)
        image += pbuf[p]
    value = image + jnp.where(left_half, noise2 * target2, 0.0)
    vrow[a] = value
    vcol[b] = value
    copies = to_row(vrow.at[a], vrow, vr_send, vr_recv)
    copies += to_col(lambda p: vcol.at[b], vcol, vc_send, vc_recv)
    for copy in copies:
        copy.start()
    sent += copies
    for p in row_peers:
        arrived(vrow, vr_recv, p)
    totals = vrow[0]
    for k in range(1, rows):
        totals += vrow[k]
    b_a_b = column(totals, 64)
    b_b = column(totals, 65)
    alpha = b_b / b_a_b

    image_r = jnp.zeros((16, cols * 64), F32)
    mean_r = jnp.zeros((16, cols * 64), F32)
    for k in range(rows):
        residual = whole(ibuf[k, 64:80, :]) - alpha * doubled(vrow[k])
        block = halves(residual)
        image_r += apply_tile(block, ktrain[k, 0:64, :], ktrain[k, 64:128, :])
        mean_r += apply_tile(block, kcand[k, 0:64, :], kcand[k, 64:128, :])
    for p in col_peers:
        arrived(vcol, vc_recv, p)
    residual_cols = over_columns(
        lambda s: whole(jbuf[s, 64:80, :]) - alpha * doubled(vcol[s])
    )
    value_own = value[:, 0:64]
    residual_own = target - alpha * value_own
    square = residual_own * residual_own
    own_rar = inner(image_r, residual_cols) + jnp.sum(noise * square, axis=1, keepdims=True)
    own_rr = jnp.sum(square, axis=1, keepdims=True)
    own_vr = jnp.sum(value_own * residual_own, axis=1, keepdims=True)
    scalars = jnp.where(
        lane == 0, own_rar, jnp.where(lane == 1, own_rr, jnp.where(lane == 2, own_vr, 0.0))
    )
    for s in range(cols):
        at = 128 * (s // 2)
        first, second = mean_b[:, at : at + 128], mean_r[:, at : at + 128]
        if s % 2:
            first = pltpu.roll(first, 64, 1)
        else:
            second = pltpu.roll(second, 64, 1)
        wsend[s, :, 0:128] = jnp.where(left_half, first, second)
        wsend[s, :, 128:256] = scalars
    copies = to_col(lambda p: wsend.at[p], wbuf, w_send, w_recv)
    for copy in copies:
        copy.start()
    sent += copies
    means = wsend[b]
    for p in col_peers:
        arrived(wbuf, w_recv, p)
        means += wbuf[p]
    scalars = means[:, 128:256]
    row_at = lax.broadcasted_iota(jnp.int32, (16, 128), 0)
    spread = jnp.zeros((16, 128), F32)
    for q in range(3):
        spread = jnp.where(lane == row_at + 16 * q, column(scalars, q), spread)
    packed = jnp.sum(spread, axis=0, keepdims=True)
    sbuf[a] = jnp.broadcast_to(packed, (8, 128))
    copies = to_row(sbuf.at[a], sbuf, s_send, s_recv)
    for copy in copies:
        copy.start()
    sent += copies
    for p in row_peers:
        arrived(sbuf, s_recv, p)
    totals = sbuf[0]
    for k in range(1, rows):
        totals += sbuf[k]
    totals = jnp.concatenate([totals, totals], axis=0)

    def unpacked(q):
        return jnp.sum(
            jnp.where(lane == row_at + 16 * q, totals, 0.0), axis=1, keepdims=True
        )

    r_a_r, fresh, v_r = unpacked(0), unpacked(1), unpacked(2)
    beta = fresh / b_b
    curve = r_a_r + 2.0 * beta * v_r + beta * beta * b_a_b
    alpha_two = fresh / curve
    share = alpha + alpha_two * beta
    solution_ref[...] = share * target + alpha_two * residual_own
    mean_ref[...] = share * means[:, 0:64] + alpha_two * means[:, 64:128]
    for copy in sent:
        copy.wait_send()


def per_device(rows, cols, train_points, cand_points, inv_length, noise, targets):
    vmem = pl.BlockSpec(memory_space=pltpu.VMEM)
    out = jax.ShapeDtypeStruct(targets.shape, F32)
    dma = pltpu.SemaphoreType.DMA
    width = cols * 64
    by_row, by_col = dma((rows,)), dma((cols,))
    return pl.pallas_call(
        functools.partial(kernel, rows, cols),
        out_shape=(out, out),
        in_specs=[vmem] * 5,
        out_specs=(vmem, vmem),
        scratch_shapes=[
            pltpu.VMEM((rows, 80, 128), BF16),
            pltpu.VMEM((cols, 80, 128), BF16),
            pltpu.VMEM((cols, 64, 128), BF16),
            pltpu.VMEM((rows, 128, width), BF16),
            pltpu.VMEM((rows, 128, width), BF16),
            pltpu.VMEM((cols, 16, 128), F32),
            pltpu.VMEM((cols, 16, 128), F32),
            pltpu.VMEM((1, 8, 128), F32),
            pltpu.VMEM((rows, 16, 128), F32),
            pltpu.VMEM((cols, 16, 128), F32),
            pltpu.VMEM((cols, 16, 256), F32),
            pltpu.VMEM((cols, 16, 256), F32),
            pltpu.VMEM((rows, 8, 128), F32),
            by_row, by_row, by_col, by_col, by_col, by_col, by_col, by_col,
            by_row, by_row, by_col, by_col, by_col, by_col, by_row, by_row,
        ],
        compiler_params=pltpu.CompilerParams(
            collective_id=0, has_side_effects=True, vmem_limit_bytes=40 * 1024 * 1024
        ),
    )(train_points, cand_points, inv_length.reshape(1, -1), noise.reshape(1, -1), targets)


def solution(mesh):
    placed = (
        P(None, ("row", "col")),
        P(None, ("row", "col")),
        P(),
        P(("row", "col")),
        P(None, ("row", "col")),
    )
    return jax.shard_map(
        functools.partial(per_device, mesh.shape["row"], mesh.shape["col"]),
        mesh=mesh,
        in_specs=placed,
        out_specs=(P(None, ("row", "col")), P(None, ("row", "col"))),
        check_vma=False,
    )
```

```python
import functools
import math

import jax
import jax.numpy as jnp
from jax import lax
from jax.experimental import pallas as pl
from jax.experimental.pallas import tpu as pltpu
from jax.sharding import PartitionSpec as P

MESH = pl.DeviceIdType.MESH
root_five = math.sqrt(5.0)
F32 = jnp.float32
BF16 = jnp.bfloat16


def lanes_of(rows):
    return lax.broadcasted_iota(jnp.int32, (rows, 128), 1)


def rounded(value):
    return value.astype(BF16).astype(F32)


def halves(doubled):
    high = rounded(doubled)
    return jnp.where(lanes_of(doubled.shape[0]) < 64, high, doubled - high).astype(BF16)


def whole(block):
    value = block.astype(F32)
    return value + pltpu.roll(value, 64, 1)


def doubled(value):
    return jnp.where(lanes_of(value.shape[0]) < 64, value, pltpu.roll(value, 64, 1))


def right_form(points):
    amount, dims = points.shape
    norm = jnp.sum(points * points, axis=1, keepdims=True)
    high = rounded(norm)
    middle = rounded(norm - high)
    low = rounded(norm - high - middle)
    lane = lanes_of(amount)
    right = jnp.concatenate([-2.0 * points, jnp.zeros((amount, 128 - dims), F32)], axis=1)
    for place, part in enumerate((high, middle, low)):
        right = jnp.where(lane == dims + place, part, right)
    return right.astype(BF16)


def right_operand(block):
    left_half = lanes_of(block.shape[0]) < 64
    value = block.astype(F32)
    return jnp.concatenate(
        [jnp.where(left_half, value, 1.0), jnp.where(left_half, 1.0, value)], axis=1
    ).astype(BF16)


def left_operand(block):
    left_half = lanes_of(block.shape[0]) < 64
    value = block.astype(F32)
    other = pltpu.roll(value, 64, 1)
    forms = []
    for here, there in ((value, other), (other, value)):
        high = rounded(there * there)
        square = here * here
        low = square - rounded(square)
        forms.append(
            jnp.concatenate(
                [jnp.where(left_half, here, high), jnp.where(left_half, low, 1.0)], axis=1
            )
        )
    return jnp.concatenate(forms, axis=0).astype(BF16)


def matern_split(left, right):
    dist = lax.dot_general(
        left, right, (((1,), (1,)), ((), ())), preferred_element_type=F32
    )
    dist = jnp.maximum(dist, 0.0)
    scaled = root_five * dist * lax.rsqrt(jnp.maximum(dist, 1e-30))
    kern = (1.0 + scaled + (5.0 / 3.0) * dist) * jnp.exp(-scaled)
    high = kern.astype(BF16)
    return high, (kern - high.astype(F32)).astype(BF16)


def pairs(slots):
    left_half = lanes_of(16) < 64
    return [
        jnp.where(left_half, slots[2 * h], slots[2 * h + 1]) for h in range(len(slots) // 2)
    ]


def rows_operand(slots):
    wide = jnp.concatenate(pairs(slots), axis=1)
    high = rounded(wide)
    return jnp.concatenate([high, wide - high], axis=0).astype(BF16)


def apply_tile(operand, high, low):
    both = jnp.dot(operand, high, preferred_element_type=F32)
    both += jnp.dot(operand, low, preferred_element_type=F32)
    return both[:16] + both[16:]


def column(value, lane_at):
    return jnp.sum(
        jnp.where(lanes_of(value.shape[0]) == lane_at, value, 0.0), axis=1, keepdims=True
    )


def kernel(
    rows, cols,
    train_hbm, cand_hbm, inv_hbm, noise_hbm, target_hbm,
    solution_ref, mean_ref,
    train_ref, cand_ref, inv_ref, noise_ref, target_ref,
    ibuf, jbuf, cbuf, train_hi, train_lo, cand_hi, cand_lo,
    psend, pbuf, vrow, vcol, wsend, wbuf, tcol, srow,
    in_sem, i_send, i_recv, j_send, j_recv, c_send, c_recv, p_send, p_recv,
    vr_send, vr_recv, vc_send, vc_recv, w_send, w_recv, t_send, t_recv, s_send, s_recv,
):
    loads = [
        pltpu.make_async_copy(src, dst, in_sem.at[n])
        for n, (src, dst) in enumerate(
            (
                (train_hbm, train_ref),
                (inv_hbm, inv_ref),
                (cand_hbm, cand_ref),
                (target_hbm, target_ref),
                (noise_hbm, noise_ref),
            )
        )
    ]
    for load in loads:
        load.start()
    a = lax.axis_index("row")
    b = lax.axis_index("col")
    row_peers = [lax.rem(a + k, rows) for k in range(1, rows)]
    col_peers = [lax.rem(b + k, cols) for k in range(1, cols)]
    order = [a] + [lax.rem(a + rows - k, rows) for k in range(1, rows)]
    group = 4
    groups = rows // group

    barrier = pltpu.get_barrier_semaphore()
    for p in row_peers:
        pl.semaphore_signal(barrier, inc=1, device_id=(p, b), device_id_type=MESH)
    for p in col_peers:
        pl.semaphore_signal(barrier, inc=1, device_id=(a, p), device_id_type=MESH)

    sent = []

    def to_row(src, buf, send, recv):
        for p in row_peers:
            copy = pltpu.make_async_remote_copy(
                src_ref=src, dst_ref=buf.at[a], send_sem=send.at[p], recv_sem=recv.at[a],
                device_id=(p, b), device_id_type=MESH,
            )
            copy.start()
            sent.append(copy)

    def to_col(src, buf, send, recv):
        for p in col_peers:
            copy = pltpu.make_async_remote_copy(
                src_ref=src(p), dst_ref=buf.at[b], send_sem=send.at[p], recv_sem=recv.at[b],
                device_id=(a, p), device_id_type=MESH,
            )
            copy.start()
            sent.append(copy)

    def arrived(buf, recv, peers):
        for p in peers:
            pltpu.make_async_remote_copy(
                src_ref=buf.at[p], dst_ref=buf.at[p], send_sem=recv.at[p], recv_sem=recv.at[p],
                device_id=(a, b), device_id_type=MESH,
            ).wait_recv()

    lane = lanes_of(16)
    left_half = lane < 64

    for load in loads:
        load.wait()
    own_points = train_ref.shape[1]
    points = jnp.concatenate([train_ref[...], cand_ref[...]], axis=1).T * inv_ref[...]
    points = rounded(points)
    own_train = points[:own_points]
    target = target_ref[...]
    target2 = jnp.concatenate([target, target], axis=1)
    target_block = halves(target2)
    noise = noise_ref[...]
    noise2 = jnp.concatenate([noise, noise], axis=1)
    ibuf[a, 0:32, :] = jnp.concatenate([own_train[:32], own_train[32:]], axis=1).astype(BF16)
    ibuf[a, 32:48, :] = target_block
    right = right_form(points)
    jbuf[b, 0:64, :] = right[:own_points]
    jbuf[b, 64:80, :] = target_block
    cbuf[b] = right[own_points:]

    pl.semaphore_wait(barrier, rows + cols - 2)
    to_row(ibuf.at[a], ibuf, i_send, i_recv)
    to_col(lambda p: jbuf.at[b], jbuf, j_send, j_recv)
    to_col(lambda p: cbuf.at[b], cbuf, c_send, c_recv)

    arrived(jbuf, j_recv, col_peers)
    right_train = right_operand(jbuf[:, 0:64, :].reshape(cols * 64, 128))

    def tile(slots, right, high_ref, low_ref, at):
        left = jnp.concatenate([left_operand(ibuf[order[k], 0:32, :]) for k in slots], axis=0)
        high, low = matern_split(left, right)
        high_ref[at : at + 64 * len(slots), :] = high
        low_ref[at : at + 64 * len(slots), :] = low

    def applied(slot_value, high_ref, low_ref):
        total = None
        for g in range(groups):
            span = slice(256 * g, 256 * g + 256)
            operand = rows_operand([slot_value(k) for k in range(group * g, group * g + group)])
            part = apply_tile(operand, high_ref[span, :], low_ref[span, :])
            total = part if total is None else total + part
        return total

    def targets_of(k):
        return whole(ibuf[order[k], 32:48, :])

    tile([0], right_train, train_hi, train_lo, 0)
    partial = None
    for g in range(groups):
        slots = list(range(max(1, group * g), group * g + group))
        arrived(ibuf, i_recv, [order[k] for k in slots])
        tile(slots, right_train, train_hi, train_lo, 64 * slots[0])
        span = slice(256 * g, 256 * g + 256)
        operand = rows_operand([targets_of(k) for k in range(group * g, group * g + group)])
        part = apply_tile(operand, train_hi[span, :], train_lo[span, :])
        partial = part if partial is None else partial + part

    def inner(wide, blocks):
        total = jnp.zeros((16, 128), F32)
        for h, block in enumerate(blocks):
            total += wide[:, 128 * h : 128 * h + 128] * block
        return jnp.sum(total, axis=1, keepdims=True)

    target_cols = [whole(jbuf[s, 64:80, :]) for s in range(cols)]
    own_bb = jnp.sum(target * target, axis=1, keepdims=True)
    own_bnb = jnp.sum(noise * target * target, axis=1, keepdims=True)
    scalars = jnp.where(
        lane == 64,
        inner(partial, pairs(target_cols)) + own_bnb,
        jnp.where(lane == 65, own_bb, 0.0),
    )
    for s in range(cols):
        piece = partial[:, 128 * (s // 2) : 128 * (s // 2) + 128]
        if s % 2:
            piece = pltpu.roll(piece, 64, 1)
        psend[s] = jnp.where(left_half, piece, scalars)
    to_col(lambda p: psend.at[p], pbuf, p_send, p_recv)

    arrived(cbuf, c_recv, col_peers)
    right_cand = right_operand(cbuf[...].reshape(cols * 64, 128))
    half = max(1, groups // 2)
    for g in range(half):
        tile(range(group * g, group * g + group), right_cand, cand_hi, cand_lo, 256 * g)

    arrived(pbuf, p_recv, col_peers)
    image = psend[b]
    for p in col_peers:
        image += pbuf[p]
    value = image + jnp.where(left_half, noise2 * target2, 0.0)
    vrow[a] = value
    vcol[b] = value
    to_row(vrow.at[a], vrow, vr_send, vr_recv)
    to_col(lambda p: vcol.at[b], vcol, vc_send, vc_recv)

    for g in range(half, groups):
        tile(range(group * g, group * g + group), right_cand, cand_hi, cand_lo, 256 * g)
    mean_b = applied(targets_of, cand_hi, cand_lo)

    arrived(vrow, vr_recv, row_peers)
    totals = vrow[0]
    for k in range(1, rows):
        totals += vrow[k]
    b_a_b = column(totals, 64)
    b_b = column(totals, 65)
    alpha = b_b / b_a_b

    def residual_of(k):
        return targets_of(k) - alpha * doubled(vrow[order[k]])

    image_r = applied(residual_of, train_hi, train_lo)
    arrived(vcol, vc_recv, col_peers)
    residual_cols = pairs([target_cols[s] - alpha * doubled(vcol[s]) for s in range(cols)])
    value_own = value[:, 0:64]
    residual_own = target - alpha * value_own
    square = residual_own * residual_own
    own_rar = inner(image_r, residual_cols) + jnp.sum(noise * square, axis=1, keepdims=True)
    own_rr = jnp.sum(square, axis=1, keepdims=True)
    own_vr = jnp.sum(value_own * residual_own, axis=1, keepdims=True)
    row_at = lax.broadcasted_iota(jnp.int32, (16, 128), 0)
    spread = jnp.where(
        lane == row_at,
        own_rar,
        jnp.where(lane == row_at + 16, own_rr, jnp.where(lane == row_at + 32, own_vr, 0.0)),
    )
    tcol[b] = jnp.broadcast_to(jnp.sum(spread, axis=0, keepdims=True), (8, 128))
    to_col(lambda p: tcol.at[b], tcol, t_send, t_recv)

    mean_r = applied(residual_of, cand_hi, cand_lo)
    for s in range(cols):
        at = 128 * (s // 2)
        first, second = mean_b[:, at : at + 128], mean_r[:, at : at + 128]
        if s % 2:
            first = pltpu.roll(first, 64, 1)
        else:
            second = pltpu.roll(second, 64, 1)
        wsend[s] = jnp.where(left_half, first, second)
    to_col(lambda p: wsend.at[p], wbuf, w_send, w_recv)

    arrived(tcol, t_recv, col_peers)
    totals = tcol[0]
    for s in range(1, cols):
        totals += tcol[s]
    srow[a] = totals
    to_row(srow.at[a], srow, s_send, s_recv)

    arrived(wbuf, w_recv, col_peers)
    means = wsend[b]
    for p in col_peers:
        means += wbuf[p]
    arrived(srow, s_recv, row_peers)
    totals = srow[0]
    for k in range(1, rows):
        totals += srow[k]
    totals = jnp.concatenate([totals, totals], axis=0)

    def unpacked(q):
        return jnp.sum(
            jnp.where(lane == row_at + 16 * q, totals, 0.0), axis=1, keepdims=True
        )

    r_a_r, fresh, v_r = unpacked(0), unpacked(1), unpacked(2)
    beta = fresh / b_b
    curve = r_a_r + 2.0 * beta * v_r + beta * beta * b_a_b
    alpha_two = fresh / curve
    share = alpha + alpha_two * beta
    solution_ref[...] = share * target + alpha_two * residual_own
    mean_ref[...] = share * means[:, 0:64] + alpha_two * means[:, 64:128]
    for copy in sent:
        copy.wait_send()


def per_device(rows, cols, train_points, cand_points, inv_length, noise, targets):
    vmem = pl.BlockSpec(memory_space=pltpu.VMEM)
    hbm = pl.BlockSpec(memory_space=pltpu.HBM)
    out = jax.ShapeDtypeStruct(targets.shape, F32)
    operands = (
        train_points, cand_points, inv_length.reshape(1, -1), noise.reshape(1, -1), targets
    )
    dma = pltpu.SemaphoreType.DMA
    width = cols * 64
    by_row, by_col = dma((rows,)), dma((cols,))
    kernel_tile = pltpu.VMEM((rows * 64, width), BF16)
    return pl.pallas_call(
        functools.partial(kernel, rows, cols),
        out_shape=(out, out),
        in_specs=[hbm] * 5,
        out_specs=(vmem, vmem),
        scratch_shapes=[pltpu.VMEM(operand.shape, F32) for operand in operands]
        + [
            pltpu.VMEM((rows, 48, 128), BF16),
            pltpu.VMEM((cols, 80, 128), BF16),
            pltpu.VMEM((cols, 64, 128), BF16),
            kernel_tile, kernel_tile, kernel_tile, kernel_tile,
            pltpu.VMEM((cols, 16, 128), F32),
            pltpu.VMEM((cols, 16, 128), F32),
            pltpu.VMEM((rows, 16, 128), F32),
            pltpu.VMEM((cols, 16, 128), F32),
            pltpu.VMEM((cols, 16, 128), F32),
            pltpu.VMEM((cols, 16, 128), F32),
            pltpu.VMEM((cols, 8, 128), F32),
            pltpu.VMEM((rows, 8, 128), F32),
            dma((5,)),
            by_row, by_row, by_col, by_col, by_col, by_col, by_col, by_col,
            by_row, by_row, by_col, by_col, by_col, by_col, by_col, by_col, by_row, by_row,
        ],
        compiler_params=pltpu.CompilerParams(
            collective_id=0, has_side_effects=True, vmem_limit_bytes=60 * 1024 * 1024
        ),
    )(*operands)


def solution(mesh):
    placed = (
        P(None, ("row", "col")),
        P(None, ("row", "col")),
        P(),
        P(("row", "col")),
        P(None, ("row", "col")),
    )
    return jax.shard_map(
        functools.partial(per_device, mesh.shape["row"], mesh.shape["col"]),
        mesh=mesh,
        in_specs=placed,
        out_specs=(P(None, ("row", "col")), P(None, ("row", "col"))),
        check_vma=False,
    )
```

```python
import functools
import math

import jax
import jax.numpy as jnp
from jax import lax
from jax.experimental import pallas as pl
from jax.experimental.pallas import tpu as pltpu
from jax.sharding import PartitionSpec as P

MESH = pl.DeviceIdType.MESH
root_five = math.sqrt(5.0)
F32 = jnp.float32
BF16 = jnp.bfloat16


def lanes_of(rows):
    return lax.broadcasted_iota(jnp.int32, (rows, 128), 1)


def rounded(value):
    return value.astype(BF16).astype(F32)


def halves(doubled):
    high = rounded(doubled)
    return jnp.where(lanes_of(doubled.shape[0]) < 64, high, doubled - high).astype(BF16)


def whole(block):
    value = block.astype(F32)
    return value + pltpu.roll(value, 64, 1)


def doubled(value):
    return jnp.where(lanes_of(value.shape[0]) < 64, value, pltpu.roll(value, 64, 1))


def right_form(points):
    amount, dims = points.shape
    norm = jnp.sum(points * points, axis=1, keepdims=True)
    high = rounded(norm)
    middle = rounded(norm - high)
    low = rounded(norm - high - middle)
    lane = lanes_of(amount)
    right = jnp.concatenate([-2.0 * points, jnp.zeros((amount, 128 - dims), F32)], axis=1)
    for place, part in enumerate((high, middle, low)):
        right = jnp.where(lane == dims + place, part, right)
    return right.astype(BF16)


def right_operand(block):
    left_half = lanes_of(block.shape[0]) < 64
    value = block.astype(F32)
    return jnp.concatenate(
        [jnp.where(left_half, value, 1.0), jnp.where(left_half, 1.0, value)], axis=1
    ).astype(BF16)


def left_operand(block):
    left_half = lanes_of(block.shape[0]) < 64
    value = block.astype(F32)
    other = pltpu.roll(value, 64, 1)
    forms = []
    for here, there in ((value, other), (other, value)):
        high = rounded(there * there)
        square = here * here
        low = square - rounded(square)
        forms.append(
            jnp.concatenate(
                [jnp.where(left_half, here, high), jnp.where(left_half, low, 1.0)], axis=1
            )
        )
    return jnp.concatenate(forms, axis=0).astype(BF16)


def matern_split(left, right):
    dist = lax.dot_general(
        left, right, (((1,), (1,)), ((), ())), preferred_element_type=F32
    )
    dist = jnp.maximum(dist, 0.0)
    scaled = root_five * dist * lax.rsqrt(jnp.maximum(dist, 1e-30))
    kern = (1.0 + scaled + (5.0 / 3.0) * dist) * jnp.exp(-scaled)
    high = kern.astype(BF16)
    return high, (kern - high.astype(F32)).astype(BF16)


def pairs(slots):
    left_half = lanes_of(16) < 64
    return [
        jnp.where(left_half, slots[2 * h], slots[2 * h + 1]) for h in range(len(slots) // 2)
    ]


def rows_operand(slots):
    wide = jnp.concatenate(pairs(slots), axis=1)
    high = rounded(wide)
    return jnp.concatenate([high, wide - high], axis=0).astype(BF16)


def apply_tile(operand, high, low):
    both = jnp.dot(operand, high, preferred_element_type=F32)
    both += jnp.dot(operand, low, preferred_element_type=F32)
    return both[:16] + both[16:]


def column(value, lane_at):
    return jnp.sum(
        jnp.where(lanes_of(value.shape[0]) == lane_at, value, 0.0), axis=1, keepdims=True
    )


def kernel(
    rows, cols,
    train_hbm, cand_hbm, inv_hbm, noise_hbm, target_hbm,
    solution_ref, mean_ref,
    train_ref, cand_ref, inv_ref, noise_ref, target_ref,
    ibuf, jbuf, cbuf, train_hi, train_lo, cand_hi, cand_lo,
    psend, pbuf, vrow, vcol, wsend, wbuf, total_ref,
    in_sem, i_send, i_recv, j_send, j_recv, c_send, c_recv, p_send, p_recv,
    vr_send, vr_recv, vc_send, vc_recv, w_send, w_recv, s_send, s_recv,
):
    loads = [
        pltpu.make_async_copy(src, dst, in_sem.at[n])
        for n, (src, dst) in enumerate(
            (
                (train_hbm, train_ref),
                (inv_hbm, inv_ref),
                (cand_hbm, cand_ref),
                (target_hbm, target_ref),
                (noise_hbm, noise_ref),
            )
        )
    ]
    for load in loads:
        load.start()
    a = lax.axis_index("row")
    b = lax.axis_index("col")
    row_peers = [lax.rem(a + k, rows) for k in range(1, rows)]
    col_peers = [lax.rem(b + k, cols) for k in range(1, cols)]
    order = [a] + [lax.rem(a + rows - k, rows) for k in range(1, rows)]
    group = 4
    groups = rows // group

    barrier = pltpu.get_barrier_semaphore()
    devices = rows * cols
    me = a * cols + b

    def each_other(act):
        def step(k, carry):
            other = lax.rem(me + k, devices)
            act((lax.div(other, cols), lax.rem(other, cols)))
            return carry

        if devices <= 64:
            for k in range(1, devices):
                step(k, 0)
        else:
            lax.fori_loop(1, devices, step, 0)

    each_other(
        lambda device: pl.semaphore_signal(
            barrier, inc=1, device_id=device, device_id_type=MESH
        )
    )

    sent = []

    def start(src, dst, send, recv, device):
        pltpu.make_async_remote_copy(
            src_ref=src, dst_ref=dst, send_sem=send, recv_sem=recv,
            device_id=device, device_id_type=MESH,
        ).start()

    def blocks(buf, amount, sem):
        span = buf.at[pl.ds(0, amount)]
        return pltpu.make_async_remote_copy(
            src_ref=span, dst_ref=span, send_sem=sem, recv_sem=sem,
            device_id=(a, b), device_id_type=MESH,
        )

    def to_row(src, buf, send, recv):
        for p in row_peers:
            start(src, buf.at[a], send, recv, (p, b))
        sent.append(blocks(buf, rows - 1, send))

    def to_col(src, buf, send, recv):
        for p in col_peers:
            start(src(p), buf.at[b], send, recv, (a, p))
        sent.append(blocks(buf, cols - 1, send))

    def all_arrived(buf, recv):
        blocks(buf, buf.shape[0] - 1, recv).wait_recv()

    lane = lanes_of(16)
    left_half = lane < 64

    for load in loads:
        load.wait()
    own_points = train_ref.shape[1]
    points = jnp.concatenate([train_ref[...], cand_ref[...]], axis=1).T * inv_ref[...]
    points = rounded(points)
    own_train = points[:own_points]
    target = target_ref[...]
    target2 = jnp.concatenate([target, target], axis=1)
    target_block = halves(target2)
    noise = noise_ref[...]
    noise2 = jnp.concatenate([noise, noise], axis=1)
    ibuf[a, 0:32, :] = jnp.concatenate([own_train[:32], own_train[32:]], axis=1).astype(BF16)
    ibuf[a, 32:48, :] = target_block
    right = right_form(points)
    jbuf[b, 0:64, :] = right[:own_points]
    jbuf[b, 64:80, :] = target_block
    cbuf[b] = right[own_points:]

    pl.semaphore_wait(barrier, devices - 1)
    for p in row_peers:
        start(ibuf.at[a], ibuf.at[a], i_send, i_recv.at[a], (p, b))
    sent.append(blocks(ibuf, rows - 1, i_send))
    to_col(lambda p: jbuf.at[b], jbuf, j_send, j_recv)
    to_col(lambda p: cbuf.at[b], cbuf, c_send, c_recv)

    all_arrived(jbuf, j_recv)
    right_train = right_operand(jbuf[:, 0:64, :].reshape(cols * 64, 128))

    def tile(slots, right, high_ref, low_ref, at):
        left = jnp.concatenate([left_operand(ibuf[order[k], 0:32, :]) for k in slots], axis=0)
        high, low = matern_split(left, right)
        high_ref[at : at + 64 * len(slots), :] = high
        low_ref[at : at + 64 * len(slots), :] = low

    def applied(slot_value, high_ref, low_ref):
        total = None
        for g in range(groups):
            span = slice(256 * g, 256 * g + 256)
            operand = rows_operand([slot_value(k) for k in range(group * g, group * g + group)])
            part = apply_tile(operand, high_ref[span, :], low_ref[span, :])
            total = part if total is None else total + part
        return total

    def targets_of(k):
        return whole(ibuf[order[k], 32:48, :])

    tile([0], right_train, train_hi, train_lo, 0)
    partial = None
    for g in range(groups):
        slots = list(range(max(1, group * g), group * g + group))
        for k in slots:
            p = order[k]
            pltpu.make_async_remote_copy(
                src_ref=ibuf.at[p], dst_ref=ibuf.at[p], send_sem=i_send, recv_sem=i_recv.at[p],
                device_id=(a, b), device_id_type=MESH,
            ).wait_recv()
        tile(slots, right_train, train_hi, train_lo, 64 * slots[0])
        span = slice(256 * g, 256 * g + 256)
        operand = rows_operand([targets_of(k) for k in range(group * g, group * g + group)])
        part = apply_tile(operand, train_hi[span, :], train_lo[span, :])
        partial = part if partial is None else partial + part

    def inner(wide, blocks):
        total = jnp.zeros((16, 128), F32)
        for h, block in enumerate(blocks):
            total += wide[:, 128 * h : 128 * h + 128] * block
        return jnp.sum(total, axis=1, keepdims=True)

    target_cols = [whole(jbuf[s, 64:80, :]) for s in range(cols)]
    own_bb = jnp.sum(target * target, axis=1, keepdims=True)
    own_bnb = jnp.sum(noise * target * target, axis=1, keepdims=True)
    scalars = jnp.where(
        lane == 64,
        inner(partial, pairs(target_cols)) + own_bnb,
        jnp.where(lane == 65, own_bb, 0.0),
    )
    for s in range(cols):
        piece = partial[:, 128 * (s // 2) : 128 * (s // 2) + 128]
        if s % 2:
            piece = pltpu.roll(piece, 64, 1)
        psend[s] = jnp.where(left_half, piece, scalars)
    to_col(lambda p: psend.at[p], pbuf, p_send, p_recv)

    all_arrived(cbuf, c_recv)
    right_cand = right_operand(cbuf[...].reshape(cols * 64, 128))
    half = max(1, groups // 2)
    for g in range(half):
        tile(range(group * g, group * g + group), right_cand, cand_hi, cand_lo, 256 * g)

    all_arrived(pbuf, p_recv)
    image = psend[b]
    for p in col_peers:
        image += pbuf[p]
    value = image + jnp.where(left_half, noise2 * target2, 0.0)
    vrow[a] = value
    vcol[b] = value
    to_row(vrow.at[a], vrow, vr_send, vr_recv)
    to_col(lambda p: vcol.at[b], vcol, vc_send, vc_recv)

    for g in range(half, groups):
        tile(range(group * g, group * g + group), right_cand, cand_hi, cand_lo, 256 * g)
    mean_b = applied(targets_of, cand_hi, cand_lo)

    all_arrived(vrow, vr_recv)
    totals = vrow[0]
    for k in range(1, rows):
        totals += vrow[k]
    b_a_b = column(totals, 64)
    b_b = column(totals, 65)
    alpha = b_b / b_a_b

    def residual_of(k):
        return targets_of(k) - alpha * doubled(vrow[order[k]])

    image_r = applied(residual_of, train_hi, train_lo)
    all_arrived(vcol, vc_recv)
    residual_cols = pairs([target_cols[s] - alpha * doubled(vcol[s]) for s in range(cols)])
    value_own = value[:, 0:64]
    residual_own = target - alpha * value_own
    square = residual_own * residual_own
    own_rar = inner(image_r, residual_cols) + jnp.sum(noise * square, axis=1, keepdims=True)
    own_rr = jnp.sum(square, axis=1, keepdims=True)
    own_vr = jnp.sum(value_own * residual_own, axis=1, keepdims=True)
    row_at = lax.broadcasted_iota(jnp.int32, (16, 128), 0)
    spread = jnp.where(
        lane == row_at,
        own_rar,
        jnp.where(lane == row_at + 16, own_rr, jnp.where(lane == row_at + 32, own_vr, 0.0)),
    )
    total_ref[me] = jnp.sum(spread, axis=0, keepdims=True)
    each_other(
        lambda device: start(total_ref.at[me], total_ref.at[me], s_send, s_recv, device)
    )
    sent.append(blocks(total_ref, devices - 1, s_send))

    mean_r = applied(residual_of, cand_hi, cand_lo)
    for s in range(cols):
        at = 128 * (s // 2)
        first, second = mean_b[:, at : at + 128], mean_r[:, at : at + 128]
        if s % 2:
            first = pltpu.roll(first, 64, 1)
        else:
            second = pltpu.roll(second, 64, 1)
        wsend[s] = jnp.where(left_half, first, second)
    to_col(lambda p: wsend.at[p], wbuf, w_send, w_recv)

    all_arrived(wbuf, w_recv)
    means = wsend[b]
    for p in col_peers:
        means += wbuf[p]
    all_arrived(total_ref, s_recv)
    totals = jnp.sum(total_ref[...], axis=0)

    def unpacked(q):
        return jnp.sum(
            jnp.where(lane == row_at + 16 * q, totals, 0.0), axis=1, keepdims=True
        )

    r_a_r, fresh, v_r = unpacked(0), unpacked(1), unpacked(2)
    beta = fresh / b_b
    curve = r_a_r + 2.0 * beta * v_r + beta * beta * b_a_b
    alpha_two = fresh / curve
    share = alpha + alpha_two * beta
    solution_ref[...] = share * target + alpha_two * residual_own
    mean_ref[...] = share * means[:, 0:64] + alpha_two * means[:, 64:128]
    for copy in sent:
        copy.wait_send()


def per_device(rows, cols, train_points, cand_points, inv_length, noise, targets):
    vmem = pl.BlockSpec(memory_space=pltpu.VMEM)
    hbm = pl.BlockSpec(memory_space=pltpu.HBM)
    out = pltpu.VMEM(targets.shape, F32)
    operands = (
        train_points, cand_points, inv_length.reshape(1, -1), noise.reshape(1, -1), targets
    )
    dma = pltpu.SemaphoreType.DMA
    width = cols * 64
    kernel_tile = pltpu.VMEM((rows * 64, width), BF16)
    return pl.pallas_call(
        functools.partial(kernel, rows, cols),
        out_shape=(out, out),
        in_specs=[hbm] * 5,
        out_specs=(vmem, vmem),
        scratch_shapes=[pltpu.VMEM(operand.shape, F32) for operand in operands]
        + [
            pltpu.VMEM((rows, 48, 128), BF16),
            pltpu.VMEM((cols, 80, 128), BF16),
            pltpu.VMEM((cols, 64, 128), BF16),
            kernel_tile, kernel_tile, kernel_tile, kernel_tile,
            pltpu.VMEM((cols, 16, 128), F32),
            pltpu.VMEM((cols, 16, 128), F32),
            pltpu.VMEM((rows, 16, 128), F32),
            pltpu.VMEM((cols, 16, 128), F32),
            pltpu.VMEM((cols, 16, 128), F32),
            pltpu.VMEM((cols, 16, 128), F32),
            pltpu.VMEM((rows * cols, 1, 128), F32),
            dma((5,)), dma, dma((rows,)),
        ]
        + [dma] * 14,
        compiler_params=pltpu.CompilerParams(
            collective_id=0, has_side_effects=True, vmem_limit_bytes=60 * 1024 * 1024
        ),
    )(*operands)


def solution(mesh):
    placed = (
        P(None, ("row", "col")),
        P(None, ("row", "col")),
        P(),
        P(("row", "col")),
        P(None, ("row", "col")),
    )
    return jax.shard_map(
        functools.partial(per_device, mesh.shape["row"], mesh.shape["col"]),
        mesh=mesh,
        in_specs=placed,
        out_specs=(P(None, ("row", "col")), P(None, ("row", "col"))),
        check_vma=False,
    )
```

```python
import functools
import math

import jax
import jax.numpy as jnp
from jax import lax
from jax.experimental import pallas as pl
from jax.experimental.pallas import tpu as pltpu
from jax.sharding import PartitionSpec as P

MESH = pl.DeviceIdType.MESH
root_five = math.sqrt(5.0)
F32 = jnp.float32
BF16 = jnp.bfloat16


def in_left(rows):
    return lax.broadcasted_iota(jnp.int32, (rows, 128), 1) < 64


def turned(value):
    return pltpu.roll(value, 64, 1)


def rounded(value):
    return value.astype(BF16).astype(F32)


def halves(doubled):
    high = rounded(doubled)
    return jnp.where(in_left(doubled.shape[0]), high, doubled - high).astype(BF16)


def whole(block):
    value = block.astype(F32)
    return value + turned(value)


def packed(wide, second):
    top, bottom = wide[0:8], wide[8:16]
    if second:
        return jnp.where(in_left(8), turned(top), bottom)
    return jnp.where(in_left(8), top, turned(bottom))


def unpacked(first, second):
    left = in_left(8)
    return jnp.concatenate(
        [jnp.where(left, first, turned(second)), jnp.where(left, turned(first), second)], axis=0
    )


def both_halves(block):
    value = block.astype(F32)
    other = turned(value)
    return (value, other), (other, value)


def squares(value):
    square = value * value
    high = rounded(square)
    return high, square - high


def left_operand(block):
    left = in_left(block.shape[0])
    forms = []
    for here, there in both_halves(block):
        high, low = squares(there)[0], squares(here)[1]
        forms.append(
            jnp.concatenate([jnp.where(left, here, high), jnp.where(left, low, 0.0)], axis=1)
        )
    return jnp.concatenate(forms, axis=0).astype(BF16)


def right_operand(blocks):
    forms, square_forms = [], []
    for block in blocks:
        left = in_left(block.shape[0])
        for here, there in both_halves(block):
            forms.append(
                jnp.concatenate(
                    [jnp.where(left, -2.0 * here, 1.0), jnp.where(left, 1.0, 0.0)], axis=1
                )
            )
            square_forms.append(jnp.where(left, squares(here)[0], squares(there)[1]))
    operand = jnp.concatenate(forms, axis=0).astype(BF16)
    summed = lax.dot_general(
        jnp.ones((16, 128), BF16),
        jnp.concatenate(square_forms, axis=0).astype(BF16),
        (((1,), (1,)), ((), ())),
        preferred_element_type=F32,
    )
    return operand, summed[0:1]


def matern_split(left, right, right_norm):
    dist = lax.dot_general(
        left, right, (((1,), (1,)), ((), ())), preferred_element_type=F32
    )
    dist = jnp.maximum(dist + right_norm, 0.0)
    scaled = root_five * dist * lax.rsqrt(jnp.maximum(dist, 1e-30))
    kern = (1.0 + scaled + (5.0 / 3.0) * dist) * jnp.exp(-scaled)
    high = kern.astype(BF16)
    return high, (kern - high.astype(F32)).astype(BF16)


def pairs(slots):
    left = in_left(16)
    return [jnp.where(left, slots[2 * h], slots[2 * h + 1]) for h in range(len(slots) // 2)]


def unpacked_pairs(slots):
    return [unpacked(slots[2 * h], slots[2 * h + 1]) for h in range(len(slots) // 2)]


def applied(blocks, high_ref, low_ref):
    total = None
    for at in range(0, len(blocks), 2):
        wide = jnp.concatenate(blocks[at : at + 2], axis=1)
        high = rounded(wide)
        operand = jnp.concatenate([high, wide - high], axis=0).astype(BF16)
        span = slice(128 * at, 128 * at + wide.shape[1])
        part = jnp.dot(operand, high_ref[span, :], preferred_element_type=F32)
        part += jnp.dot(operand, low_ref[span, :], preferred_element_type=F32)
        total = part if total is None else total + part
    return total[:16] + total[16:]


def kernel(
    rows, cols,
    train_hbm, cand_hbm, inv_hbm, noise_hbm, target_hbm,
    solution_ref, mean_ref,
    train_ref, cand_ref, inv_ref, noise_ref, target_ref,
    lbuf, pbuf, cbuf, train_hi, train_lo, cand_hi, cand_lo,
    image_send, image_buf, vline, vplane, wsend, wbuf, first_ref, last_ref,
    in_sem, l_recv,
    l_send, p_send, p_recv, c_send, c_recv, image_out, image_in,
    vl_send, vl_recv, vp_send, vp_recv, w_send, w_recv,
    first_send, first_recv, last_send, last_recv,
):
    loads = [
        pltpu.make_async_copy(src, dst, in_sem.at[n])
        for n, (src, dst) in enumerate(
            (
                (train_hbm, train_ref),
                (inv_hbm, inv_ref),
                (target_hbm, target_ref),
                (cand_hbm, cand_ref),
                (noise_hbm, noise_ref),
            )
        )
    ]
    for load in loads:
        load.start()
    a = lax.axis_index("row")
    b = lax.axis_index("col")
    devices = rows * cols
    me = a * cols + b
    z, core = lax.div(a, 2), lax.rem(a, 2)
    line, plane = rows // 2, 2 * cols
    spot = core * cols + b
    line_peers = [lax.rem(z + k, line) for k in range(1, line)]
    plane_peers = [lax.rem(spot + k, plane) for k in range(1, plane)]
    order = [z] + [lax.rem(z + line - k, line) for k in range(1, line)]

    def each_other(act):
        def step(k, carry):
            other = lax.rem(me + k, devices)
            act((lax.div(other, cols), lax.rem(other, cols)))
            return carry

        if devices <= 64:
            for k in range(1, devices):
                step(k, 0)
        else:
            lax.fori_loop(1, devices, step, 0)

    barrier = pltpu.get_barrier_semaphore()
    each_other(
        lambda device: pl.semaphore_signal(
            barrier, inc=1, device_id=device, device_id_type=MESH
        )
    )

    sent = []

    def start(src, dst, send, recv, device):
        pltpu.make_async_remote_copy(
            src_ref=src, dst_ref=dst, send_sem=send, recv_sem=recv,
            device_id=device, device_id_type=MESH,
        ).start()

    def blocks(buf, amount, sem):
        span = buf.at[pl.ds(0, amount)]
        return pltpu.make_async_remote_copy(
            src_ref=span, dst_ref=span, send_sem=sem, recv_sem=sem,
            device_id=(a, b), device_id_type=MESH,
        )

    def to_line(src, buf, send, recv):
        for p in line_peers:
            start(src, buf.at[z], send, recv, (2 * p + core, b))
        sent.append(blocks(buf, line - 1, send))

    def to_plane(src, buf, send, recv):
        for p in plane_peers:
            device = (2 * z + lax.div(p, cols), lax.rem(p, cols))
            start(src(p), buf.at[spot], send, recv, device)
        sent.append(blocks(buf, plane - 1, send))

    def to_all(buf, send, recv):
        each_other(lambda device: start(buf.at[me], buf.at[me], send, recv, device))
        sent.append(blocks(buf, devices - 1, send))

    def arrived(buf, recv):
        blocks(buf, buf.shape[0] - 1, recv).wait_recv()

    lane = lax.broadcasted_iota(jnp.int32, (16, 128), 1)
    row_at = lax.broadcasted_iota(jnp.int32, (16, 128), 0)
    left16 = lane < 64

    def points_of(ref):
        scaled = rounded(ref[...].T * inv_ref[...])
        return jnp.concatenate([scaled[:32], scaled[32:]], axis=1).astype(BF16)

    def spread(columns):
        total = jnp.zeros((16, 128), F32)
        for q, one in enumerate(columns):
            total = jnp.where(lane == row_at + 16 * q, one, total)
        return jnp.sum(total, axis=0, keepdims=True)

    def gathered(ref, amount):
        total = jnp.sum(ref[...], axis=0)
        return [
            jnp.sum(jnp.where(lane == row_at + 16 * q, total, 0.0), axis=1, keepdims=True)
            for q in range(amount)
        ]

    def inner(wide, lane_blocks):
        total = jnp.zeros((16, 128), F32)
        for h, block in enumerate(lane_blocks):
            total += wide[:, 128 * h : 128 * h + 128] * block
        return jnp.sum(total, axis=1, keepdims=True)

    for load in loads[:3]:
        load.wait()
    target = target_ref[...]
    target2 = jnp.concatenate([target, target], axis=1)
    target_block = halves(target2)
    own_train = points_of(train_ref)
    lbuf[z, 0:32, :] = own_train
    lbuf[z, 32:48, :] = target_block
    pbuf[spot, 0:32, :] = own_train
    pbuf[spot, 32:48, :] = target_block
    pl.semaphore_wait(barrier, devices - 1)
    for p in line_peers:
        start(lbuf.at[z], lbuf.at[z], l_send, l_recv.at[z], (2 * p + core, b))
    sent.append(blocks(lbuf, line - 1, l_send))
    to_plane(lambda p: pbuf.at[spot], pbuf, p_send, p_recv)
    loads[3].wait()
    cbuf[spot] = points_of(cand_ref)
    to_plane(lambda p: cbuf.at[spot], cbuf, c_send, c_recv)
    loads[4].wait()
    noise = noise_ref[...]
    noise2 = jnp.concatenate([noise, noise], axis=1)

    def tile(slots, right, right_norm, high_ref, low_ref):
        left = jnp.concatenate([left_operand(lbuf[order[k], 0:32, :]) for k in slots], axis=0)
        span = slice(64 * slots[0], 64 * slots[0] + 64 * len(slots))
        high_ref[span, :], low_ref[span, :] = matern_split(left, right, right_norm)

    arrived(pbuf, p_recv)
    right_train, train_norm = right_operand([pbuf[s, 0:32, :] for s in range(plane)])
    tile([0], right_train, train_norm, train_hi, train_lo)
    for at in range(0, line, 4):
        slots = list(range(max(1, at), min(line, at + 4)))
        for k in slots:
            p = order[k]
            pltpu.make_async_remote_copy(
                src_ref=lbuf.at[p], dst_ref=lbuf.at[p], send_sem=l_send, recv_sem=l_recv.at[p],
                device_id=(a, b), device_id_type=MESH,
            ).wait_recv()
        tile(slots, right_train, train_norm, train_hi, train_lo)
    target_line = pairs([whole(lbuf[order[k], 32:48, :]) for k in range(line)])
    partial = applied(target_line, train_hi, train_lo)
    for s in range(plane):
        image_send[s] = packed(partial[:, 128 * (s // 2) : 128 * (s // 2) + 128], s % 2)
    to_plane(lambda p: image_send.at[p], image_buf, image_out, image_in)

    target_plane = pairs([whole(pbuf[s, 32:48, :]) for s in range(plane)])
    own_bb = jnp.sum(target * target, axis=1, keepdims=True)
    own_bnb = jnp.sum(noise * target * target, axis=1, keepdims=True)
    first_ref[me] = spread([inner(partial, target_plane) + own_bnb, own_bb])
    to_all(first_ref, first_send, first_recv)

    arrived(cbuf, c_recv)
    right_cand, cand_norm = right_operand([cbuf[s] for s in range(plane)])
    chunk = min(4, line // 2)
    chunks = [list(range(at, at + chunk)) for at in range(0, line, chunk)]
    half = len(chunks) // 2
    for slots in chunks[:half]:
        tile(slots, right_cand, cand_norm, cand_hi, cand_lo)

    arrived(image_buf, image_in)
    image = image_send[spot]
    for p in plane_peers:
        image += image_buf[p]
    left8 = in_left(8)
    target_packed = jnp.where(left8, target2[0:8], target2[8:16])
    value = image + noise2 * target_packed
    vline[z] = value
    vplane[spot] = value
    to_line(vline.at[z], vline, vl_send, vl_recv)
    to_plane(lambda p: vplane.at[spot], vplane, vp_send, vp_recv)

    for slots in chunks[half:]:
        tile(slots, right_cand, cand_norm, cand_hi, cand_lo)
    mean_b = applied(target_line, cand_hi, cand_lo)

    arrived(first_ref, first_recv)
    b_a_b, b_b = gathered(first_ref, 2)
    alpha = b_b / b_a_b

    def residuals(target_blocks, slots):
        return [
            block - alpha * values for block, values in zip(target_blocks, unpacked_pairs(slots))
        ]

    arrived(vline, vl_recv)
    residual_line = residuals(target_line, [vline[order[k]] for k in range(line)])
    image_r = applied(residual_line, train_hi, train_lo)
    arrived(vplane, vp_recv)
    residual_plane = residuals(target_plane, [vplane[s] for s in range(plane)])
    value_own = unpacked(value, value)[:, 0:64]
    residual_own = target - alpha * value_own
    square = residual_own * residual_own
    own_rar = inner(image_r, residual_plane) + jnp.sum(noise * square, axis=1, keepdims=True)
    own_rr = jnp.sum(square, axis=1, keepdims=True)
    own_vr = jnp.sum(value_own * residual_own, axis=1, keepdims=True)
    last_ref[me] = spread([own_rar, own_rr, own_vr])
    to_all(last_ref, last_send, last_recv)

    mean_r = applied(residual_line, cand_hi, cand_lo)
    for s in range(plane):
        at = 128 * (s // 2)
        first, second = mean_b[:, at : at + 128], mean_r[:, at : at + 128]
        if s % 2:
            first = turned(first)
        else:
            second = turned(second)
        wsend[s] = jnp.where(left16, first, second)
    to_plane(lambda p: wsend.at[p], wbuf, w_send, w_recv)

    arrived(wbuf, w_recv)
    means = wsend[spot]
    for p in plane_peers:
        means += wbuf[p]
    arrived(last_ref, last_recv)
    r_a_r, fresh, v_r = gathered(last_ref, 3)
    beta = fresh / b_b
    curve = r_a_r + 2.0 * beta * v_r + beta * beta * b_a_b
    alpha_two = fresh / curve
    share = alpha + alpha_two * beta
    solution_ref[...] = share * target + alpha_two * residual_own
    mean_ref[...] = share * means[:, 0:64] + alpha_two * means[:, 64:128]
    for copy in sent:
        copy.wait_send()


def per_device(rows, cols, train_points, cand_points, inv_length, noise, targets):
    vmem = pl.BlockSpec(memory_space=pltpu.VMEM)
    hbm = pl.BlockSpec(memory_space=pltpu.HBM)
    out = pltpu.VMEM(targets.shape, F32)
    operands = (
        train_points, cand_points, inv_length.reshape(1, -1), noise.reshape(1, -1), targets
    )
    dma = pltpu.SemaphoreType.DMA
    line, plane = rows // 2, 2 * cols
    kernel_tile = pltpu.VMEM((line * 64, plane * 64), BF16)
    return pl.pallas_call(
        functools.partial(kernel, rows, cols),
        out_shape=(out, out),
        in_specs=[hbm] * 5,
        out_specs=(vmem, vmem),
        scratch_shapes=[pltpu.VMEM(operand.shape, F32) for operand in operands]
        + [
            pltpu.VMEM((line, 48, 128), BF16),
            pltpu.VMEM((plane, 48, 128), BF16),
            pltpu.VMEM((plane, 32, 128), BF16),
            kernel_tile, kernel_tile, kernel_tile, kernel_tile,
            pltpu.VMEM((plane, 8, 128), F32),
            pltpu.VMEM((plane, 8, 128), F32),
            pltpu.VMEM((line, 8, 128), F32),
            pltpu.VMEM((plane, 8, 128), F32),
            pltpu.VMEM((plane, 16, 128), F32),
            pltpu.VMEM((plane, 16, 128), F32),
            pltpu.VMEM((rows * cols, 1, 128), F32),
            pltpu.VMEM((rows * cols, 1, 128), F32),
            dma((5,)), dma((line,)),
        ]
        + [dma] * 17,
        compiler_params=pltpu.CompilerParams(
            collective_id=0, has_side_effects=True, vmem_limit_bytes=60 * 1024 * 1024
        ),
    )(*operands)


def solution(mesh):
    placed = (
        P(None, ("row", "col")),
        P(None, ("row", "col")),
        P(),
        P(("row", "col")),
        P(None, ("row", "col")),
    )
    return jax.shard_map(
        functools.partial(per_device, mesh.shape["row"], mesh.shape["col"]),
        mesh=mesh,
        in_specs=placed,
        out_specs=(P(None, ("row", "col")), P(None, ("row", "col"))),
        check_vma=False,
    )
```

```python
import functools
import math

import jax
import jax.numpy as jnp
from jax import lax
from jax.experimental import pallas as pl
from jax.experimental.pallas import tpu as pltpu
from jax.sharding import PartitionSpec as P

MESH = pl.DeviceIdType.MESH
root_five = math.sqrt(5.0)
F32 = jnp.float32
BF16 = jnp.bfloat16


def in_left(rows):
    return lax.broadcasted_iota(jnp.int32, (rows, 128), 1) < 64


def turned(value):
    return pltpu.roll(value, 64, 1)


def rounded(value):
    return value.astype(BF16).astype(F32)


def halves(doubled):
    high = rounded(doubled)
    return jnp.where(in_left(doubled.shape[0]), high, doubled - high).astype(BF16)


def whole(block):
    value = block.astype(F32)
    return value + turned(value)


def packed(wide, second):
    top, bottom = wide[0:8], wide[8:16]
    if second:
        return jnp.where(in_left(8), turned(top), bottom)
    return jnp.where(in_left(8), top, turned(bottom))


def unpacked(first, second):
    left = in_left(8)
    return jnp.concatenate(
        [jnp.where(left, first, turned(second)), jnp.where(left, turned(first), second)], axis=0
    )


def both_halves(block):
    value = block.astype(F32)
    other = turned(value)
    return (value, other), (other, value)


def squares(value):
    square = value * value
    high = rounded(square)
    return high, square - high


def left_operand(block):
    left = in_left(block.shape[0])
    forms = []
    for here, there in both_halves(block):
        high, low = squares(there)[0], squares(here)[1]
        forms.append(
            jnp.concatenate([jnp.where(left, here, high), jnp.where(left, low, 0.0)], axis=1)
        )
    return jnp.concatenate(forms, axis=0).astype(BF16)


def right_operand(blocks):
    forms, square_forms = [], []
    for block in blocks:
        left = in_left(block.shape[0])
        for here, there in both_halves(block):
            forms.append(
                jnp.concatenate(
                    [jnp.where(left, -2.0 * here, 1.0), jnp.where(left, 1.0, 0.0)], axis=1
                )
            )
            square_forms.append(jnp.where(left, squares(here)[0], squares(there)[1]))
    operand = jnp.concatenate(forms, axis=0).astype(BF16)
    summed = lax.dot_general(
        jnp.ones((16, 128), BF16),
        jnp.concatenate(square_forms, axis=0).astype(BF16),
        (((1,), (1,)), ((), ())),
        preferred_element_type=F32,
    )
    return operand, summed[0:1]


def matern_split(left, right, right_norm, high_ref, low_ref, at):
    inner = lax.dot_general(
        left, right, (((1,), (1,)), ((), ())), preferred_element_type=F32
    )
    for row in range(0, inner.shape[0], 16):
        dist = jnp.maximum(inner[row : row + 16] + right_norm, 0.0)
        scaled = root_five * dist * lax.rsqrt(jnp.maximum(dist, 1e-30))
        kern = (1.0 + scaled + (5.0 / 3.0) * dist) * jnp.exp(-scaled)
        high = kern.astype(BF16)
        high_ref[at + row : at + row + 16, :] = high
        low_ref[at + row : at + row + 16, :] = (kern - high.astype(F32)).astype(BF16)


def pairs(slots):
    left = in_left(16)
    return [jnp.where(left, slots[2 * h], slots[2 * h + 1]) for h in range(len(slots) // 2)]


def unpacked_pairs(slots):
    return [unpacked(slots[2 * h], slots[2 * h + 1]) for h in range(len(slots) // 2)]


def applied(blocks, high_ref, low_ref):
    total = None
    for at in range(0, len(blocks), 2):
        wide = jnp.concatenate(blocks[at : at + 2], axis=1)
        high = rounded(wide)
        operand = jnp.concatenate([high, wide - high], axis=0).astype(BF16)
        span = slice(128 * at, 128 * at + wide.shape[1])
        part = jnp.dot(operand, high_ref[span, :], preferred_element_type=F32)
        part += jnp.dot(operand, low_ref[span, :], preferred_element_type=F32)
        total = part if total is None else total + part
    return total[:16] + total[16:]


def kernel(
    rows, cols,
    train_hbm, cand_hbm, inv_hbm, noise_hbm, target_hbm,
    out_ref,
    train_ref, cand_ref, inv_ref, noise_ref, target_ref,
    lbuf, pbuf, cbuf, train_hi, train_lo, cand_hi, cand_lo,
    image_send, image_buf, vline, vplane, wsend, wbuf, first_ref, last_ref,
    in_sem, l_recv,
    l_send, p_send, p_recv, c_send, c_recv, image_out, image_in,
    vl_send, vl_recv, vp_send, vp_recv, w_send, w_recv,
    first_send, first_recv, last_send, last_recv,
):
    loads = [
        pltpu.make_async_copy(src, dst, in_sem.at[n])
        for n, (src, dst) in enumerate(
            (
                (train_hbm, train_ref),
                (inv_hbm, inv_ref),
                (target_hbm, target_ref),
                (cand_hbm, cand_ref),
                (noise_hbm, noise_ref),
            )
        )
    ]
    for load in loads:
        load.start()
    a = lax.axis_index("row")
    b = lax.axis_index("col")
    devices = rows * cols
    me = a * cols + b
    z, core = lax.div(a, 2), lax.rem(a, 2)
    line, plane = rows // 2, 2 * cols
    spot = core * cols + b
    line_peers = [lax.rem(z + k, line) for k in range(1, line)]
    plane_peers = [lax.rem(spot + k, plane) for k in range(1, plane)]
    order = [z] + [lax.rem(z + line - k, line) for k in range(1, line)]

    def each_other(act):
        def step(k, carry):
            other = lax.rem(me + k, devices)
            act((lax.div(other, cols), lax.rem(other, cols)))
            return carry

        if devices <= 64:
            for k in range(1, devices):
                step(k, 0)
        else:
            lax.fori_loop(1, devices, step, 0)

    barrier = pltpu.get_barrier_semaphore()
    each_other(
        lambda device: pl.semaphore_signal(
            barrier, inc=1, device_id=device, device_id_type=MESH
        )
    )

    sent = []

    def start(src, dst, send, recv, device):
        pltpu.make_async_remote_copy(
            src_ref=src, dst_ref=dst, send_sem=send, recv_sem=recv,
            device_id=device, device_id_type=MESH,
        ).start()

    def blocks(buf, amount, sem):
        span = buf.at[pl.ds(0, amount)]
        return pltpu.make_async_remote_copy(
            src_ref=span, dst_ref=span, send_sem=sem, recv_sem=sem,
            device_id=(a, b), device_id_type=MESH,
        )

    def to_line(src, buf, send, recv):
        for p in line_peers:
            start(src, buf.at[z], send, recv, (2 * p + core, b))
        sent.append(blocks(buf, line - 1, send))

    def to_plane(src, buf, send, recv):
        for p in plane_peers:
            device = (2 * z + lax.div(p, cols), lax.rem(p, cols))
            start(src(p), buf.at[spot], send, recv, device)
        sent.append(blocks(buf, plane - 1, send))

    def to_all(buf, send, recv):
        each_other(lambda device: start(buf.at[me], buf.at[me], send, recv, device))
        sent.append(blocks(buf, devices - 1, send))

    def arrived(buf, recv):
        blocks(buf, buf.shape[0] - 1, recv).wait_recv()

    lane = lax.broadcasted_iota(jnp.int32, (16, 128), 1)
    row_at = lax.broadcasted_iota(jnp.int32, (16, 128), 0)
    left16 = lane < 64

    def points_of(ref):
        scaled = rounded(ref[...].T * inv_ref[...])
        return jnp.concatenate([scaled[:32], scaled[32:]], axis=1).astype(BF16)

    def spread(columns):
        total = jnp.zeros((16, 128), F32)
        for q, one in enumerate(columns):
            total = jnp.where(lane == row_at + 16 * q, one, total)
        return jnp.sum(total, axis=0, keepdims=True)

    def gathered(ref, amount):
        total = jnp.sum(ref[...], axis=0)
        return [
            jnp.sum(jnp.where(lane == row_at + 16 * q, total, 0.0), axis=1, keepdims=True)
            for q in range(amount)
        ]

    def inner(wide, lane_blocks):
        total = jnp.zeros((16, 128), F32)
        for h, block in enumerate(lane_blocks):
            total += wide[:, 128 * h : 128 * h + 128] * block
        return jnp.sum(total, axis=1, keepdims=True)

    for load in loads[:3]:
        load.wait()
    target = target_ref[...]
    target2 = jnp.concatenate([target, target], axis=1)
    target_block = halves(target2)
    own_train = points_of(train_ref)
    lbuf[z, 0:32, :] = own_train
    lbuf[z, 32:48, :] = target_block
    pbuf[spot, 0:32, :] = own_train
    pbuf[spot, 32:48, :] = target_block
    pl.semaphore_wait(barrier, devices - 1)
    for p in line_peers:
        start(lbuf.at[z], lbuf.at[z], l_send, l_recv.at[z], (2 * p + core, b))
    sent.append(blocks(lbuf, line - 1, l_send))
    to_plane(lambda p: pbuf.at[spot], pbuf, p_send, p_recv)
    loads[3].wait()
    cbuf[spot] = points_of(cand_ref)
    to_plane(lambda p: cbuf.at[spot], cbuf, c_send, c_recv)
    loads[4].wait()
    noise = noise_ref[...]
    noise2 = jnp.concatenate([noise, noise], axis=1)

    def tile(slots, right, right_norm, high_ref, low_ref):
        left = jnp.concatenate([left_operand(lbuf[order[k], 0:32, :]) for k in slots], axis=0)
        matern_split(left, right, right_norm, high_ref, low_ref, 64 * slots[0])

    arrived(pbuf, p_recv)
    right_train, train_norm = right_operand([pbuf[s, 0:32, :] for s in range(plane)])
    tile([0], right_train, train_norm, train_hi, train_lo)
    for at in range(0, line, 4):
        slots = list(range(max(1, at), min(line, at + 4)))
        for k in slots:
            p = order[k]
            pltpu.make_async_remote_copy(
                src_ref=lbuf.at[p], dst_ref=lbuf.at[p], send_sem=l_send, recv_sem=l_recv.at[p],
                device_id=(a, b), device_id_type=MESH,
            ).wait_recv()
        tile(slots, right_train, train_norm, train_hi, train_lo)
    target_line = pairs([whole(lbuf[order[k], 32:48, :]) for k in range(line)])
    partial = applied(target_line, train_hi, train_lo)
    for s in range(plane):
        image_send[s] = packed(partial[:, 128 * (s // 2) : 128 * (s // 2) + 128], s % 2)
    to_plane(lambda p: image_send.at[p], image_buf, image_out, image_in)

    target_plane = pairs([whole(pbuf[s, 32:48, :]) for s in range(plane)])
    own_bb = jnp.sum(target * target, axis=1, keepdims=True)
    own_bnb = jnp.sum(noise * target * target, axis=1, keepdims=True)
    first_ref[me] = spread([inner(partial, target_plane) + own_bnb, own_bb])
    to_all(first_ref, first_send, first_recv)

    arrived(image_buf, image_in)
    image = image_send[spot]
    for p in plane_peers:
        image += image_buf[p]
    left8 = in_left(8)
    target_packed = jnp.where(left8, target2[0:8], target2[8:16])
    value = image + noise2 * target_packed
    vline[z] = value
    vplane[spot] = value
    to_line(vline.at[z], vline, vl_send, vl_recv)
    to_plane(lambda p: vplane.at[spot], vplane, vp_send, vp_recv)

    arrived(cbuf, c_recv)
    right_cand, cand_norm = right_operand([cbuf[s] for s in range(plane)])
    for at in range(0, line, 4):
        tile(list(range(at, min(line, at + 4))), right_cand, cand_norm, cand_hi, cand_lo)
    mean_b = applied(target_line, cand_hi, cand_lo)

    arrived(first_ref, first_recv)
    b_a_b, b_b = gathered(first_ref, 2)
    alpha = b_b / b_a_b

    def residuals(target_blocks, slots):
        return [
            block - alpha * values for block, values in zip(target_blocks, unpacked_pairs(slots))
        ]

    arrived(vline, vl_recv)
    residual_line = residuals(target_line, [vline[order[k]] for k in range(line)])
    image_r = applied(residual_line, train_hi, train_lo)
    mean_r = applied(residual_line, cand_hi, cand_lo)
    for s in range(plane):
        at = 128 * (s // 2)
        first, second = mean_b[:, at : at + 128], mean_r[:, at : at + 128]
        if s % 2:
            first = turned(first)
        else:
            second = turned(second)
        wsend[s] = jnp.where(left16, first, second)
    arrived(vplane, vp_recv)
    residual_plane = residuals(target_plane, [vplane[s] for s in range(plane)])
    value_own = unpacked(value, value)[:, 0:64]
    residual_own = target - alpha * value_own
    square = residual_own * residual_own
    own_rar = inner(image_r, residual_plane) + jnp.sum(noise * square, axis=1, keepdims=True)
    own_rr = jnp.sum(square, axis=1, keepdims=True)
    own_vr = jnp.sum(value_own * residual_own, axis=1, keepdims=True)
    last_ref[me] = spread([own_rar, own_rr, own_vr])
    to_plane(lambda p: wsend.at[p], wbuf, w_send, w_recv)
    to_all(last_ref, last_send, last_recv)

    arrived(wbuf, w_recv)
    means = wsend[spot]
    for p in plane_peers:
        means += wbuf[p]
    arrived(last_ref, last_recv)
    r_a_r, fresh, v_r = gathered(last_ref, 3)
    beta = fresh / b_b
    curve = r_a_r + 2.0 * beta * v_r + beta * beta * b_a_b
    alpha_two = fresh / curve
    share = alpha + alpha_two * beta
    out_ref[0:16, :] = share * target + alpha_two * residual_own
    out_ref[16:32, :] = share * means[:, 0:64] + alpha_two * means[:, 64:128]
    for copy in sent:
        copy.wait_send()


def per_device(rows, cols, train_points, cand_points, inv_length, noise, targets):
    vmem = pl.BlockSpec(memory_space=pltpu.VMEM)
    hbm = pl.BlockSpec(memory_space=pltpu.HBM)
    out = pltpu.VMEM((2 * targets.shape[0], targets.shape[1]), F32)
    operands = (
        train_points, cand_points, inv_length.reshape(1, -1), noise.reshape(1, -1), targets
    )
    dma = pltpu.SemaphoreType.DMA
    line, plane = rows // 2, 2 * cols
    kernel_tile = pltpu.VMEM((line * 64, plane * 64), BF16)
    both = pl.pallas_call(
        functools.partial(kernel, rows, cols),
        out_shape=out,
        in_specs=[hbm] * 5,
        out_specs=vmem,
        scratch_shapes=[pltpu.VMEM(operand.shape, F32) for operand in operands]
        + [
            pltpu.VMEM((line, 48, 128), BF16),
            pltpu.VMEM((plane, 48, 128), BF16),
            pltpu.VMEM((plane, 32, 128), BF16),
            kernel_tile, kernel_tile, kernel_tile, kernel_tile,
            pltpu.VMEM((plane, 8, 128), F32),
            pltpu.VMEM((plane, 8, 128), F32),
            pltpu.VMEM((line, 8, 128), F32),
            pltpu.VMEM((plane, 8, 128), F32),
            pltpu.VMEM((plane, 16, 128), F32),
            pltpu.VMEM((plane, 16, 128), F32),
            pltpu.VMEM((rows * cols, 1, 128), F32),
            pltpu.VMEM((rows * cols, 1, 128), F32),
            dma((5,)), dma((line,)),
        ]
        + [dma] * 17,
        compiler_params=pltpu.CompilerParams(
            collective_id=0, has_side_effects=True, vmem_limit_bytes=60 * 1024 * 1024
        ),
    )(*operands)
    return both[:16], both[16:]


def solution(mesh):
    placed = (
        P(None, ("row", "col")),
        P(None, ("row", "col")),
        P(),
        P(("row", "col")),
        P(None, ("row", "col")),
    )
    return jax.shard_map(
        functools.partial(per_device, mesh.shape["row"], mesh.shape["col"]),
        mesh=mesh,
        in_specs=placed,
        out_specs=(P(None, ("row", "col")), P(None, ("row", "col"))),
        check_vma=False,
    )
```

```python
import functools
import math

import jax
import jax.numpy as jnp
from jax import lax
from jax.experimental import pallas as pl
from jax.experimental.pallas import tpu as pltpu
from jax.sharding import PartitionSpec as P

LOGICAL = pl.DeviceIdType.LOGICAL
root_five = math.sqrt(5.0)
F32 = jnp.float32
BF16 = jnp.bfloat16


def in_left(rows):
    return lax.broadcasted_iota(jnp.int32, (rows, 128), 1) < 64


def turned(value):
    return pltpu.roll(value, 64, 1)


def rounded(value):
    return value.astype(BF16).astype(F32)


def halves(doubled):
    high = rounded(doubled)
    return jnp.where(in_left(doubled.shape[0]), high, doubled - high).astype(BF16)


def whole(block):
    value = block.astype(F32)
    return value + turned(value)


def packed(wide, second):
    top, bottom = wide[0:8], wide[8:16]
    if second:
        return jnp.where(in_left(8), turned(top), bottom)
    return jnp.where(in_left(8), top, turned(bottom))


def unpacked(first, second):
    left = in_left(8)
    return jnp.concatenate(
        [jnp.where(left, first, turned(second)), jnp.where(left, turned(first), second)], axis=0
    )


def both_halves(block):
    value = block.astype(F32)
    other = turned(value)
    return (value, other), (other, value)


def squares(value):
    square = value * value
    high = rounded(square)
    return high, square - high


def left_operand(block):
    left = in_left(block.shape[0])
    forms = []
    for here, there in both_halves(block):
        high, low = squares(there)[0], squares(here)[1]
        forms.append(
            jnp.concatenate([jnp.where(left, here, high), jnp.where(left, low, 0.0)], axis=1)
        )
    return jnp.concatenate(forms, axis=0).astype(BF16)


def right_operand(blocks):
    forms, square_forms = [], []
    for block in blocks:
        left = in_left(block.shape[0])
        for here, there in both_halves(block):
            forms.append(
                jnp.concatenate(
                    [jnp.where(left, -2.0 * here, 1.0), jnp.where(left, 1.0, 0.0)], axis=1
                )
            )
            square_forms.append(jnp.where(left, squares(here)[0], squares(there)[1]))
    operand = jnp.concatenate(forms, axis=0).astype(BF16)
    summed = lax.dot_general(
        jnp.ones((16, 128), BF16),
        jnp.concatenate(square_forms, axis=0).astype(BF16),
        (((1,), (1,)), ((), ())),
        preferred_element_type=F32,
    )
    return operand, summed[0:1]


def matern_split(left, right, right_norm, high_ref, low_ref, at):
    inner = lax.dot_general(
        left, right, (((1,), (1,)), ((), ())), preferred_element_type=F32
    )
    for row in range(0, inner.shape[0], 16):
        dist = jnp.maximum(inner[row : row + 16] + right_norm, 0.0)
        scaled = root_five * dist * lax.rsqrt(jnp.maximum(dist, 1e-30))
        kern = (1.0 + scaled + (5.0 / 3.0) * dist) * jnp.exp(-scaled)
        high = kern.astype(BF16)
        high_ref[at + row : at + row + 16, :] = high
        low_ref[at + row : at + row + 16, :] = (kern - high.astype(F32)).astype(BF16)


def pairs(slots):
    left = in_left(16)
    return [jnp.where(left, slots[2 * h], slots[2 * h + 1]) for h in range(len(slots) // 2)]


def unpacked_pairs(slots):
    return [unpacked(slots[2 * h], slots[2 * h + 1]) for h in range(len(slots) // 2)]


def applied(blocks, high_ref, low_ref):
    total = None
    for at in range(0, len(blocks), 2):
        wide = jnp.concatenate(blocks[at : at + 2], axis=1)
        high = rounded(wide)
        operand = jnp.concatenate([high, wide - high], axis=0).astype(BF16)
        span = slice(128 * at, 128 * at + wide.shape[1])
        part = jnp.dot(operand, high_ref[span, :], preferred_element_type=F32)
        part += jnp.dot(operand, low_ref[span, :], preferred_element_type=F32)
        total = part if total is None else total + part
    return total[:16] + total[16:]


def kernel(
    rows, cols,
    train_hbm, cand_hbm, inv_hbm, noise_hbm, target_hbm,
    out_ref,
    train_ref, cand_ref, inv_ref, noise_ref, target_ref,
    lbuf, pbuf, cbuf, train_hi, train_lo, cand_hi, cand_lo,
    image_send, image_buf, vline, vplane, wsend, wbuf, first_ref, last_ref,
    in_sem, l_recv,
    l_send, p_send, p_recv, c_send, c_recv, image_out, image_in,
    vl_send, vl_recv, vp_send, vp_recv, w_send, w_recv,
    first_send, first_recv, last_send, last_recv,
):
    loads = [
        pltpu.make_async_copy(src, dst, in_sem.at[n])
        for n, (src, dst) in enumerate(
            (
                (train_hbm, train_ref),
                (inv_hbm, inv_ref),
                (target_hbm, target_ref),
                (cand_hbm, cand_ref),
                (noise_hbm, noise_ref),
            )
        )
    ]
    for load in loads:
        load.start()
    a = lax.axis_index("row")
    b = lax.axis_index("col")
    devices = rows * cols
    line, plane = rows // 2, 2 * cols
    z = lax.div(a, 2)
    spot = lax.rem(a, 2) * cols + b
    me = z * plane + spot
    line_peers = [lax.rem(z + k, line) for k in range(1, line)]
    plane_peers = [lax.rem(spot + k, plane) for k in range(1, plane)]
    order = [z] + [lax.rem(z + line - k, line) for k in range(1, line)]

    apart = sorted(range(1, devices), key=lambda k: abs(k - devices // 2))

    def each_other(act):
        def step(k, carry):
            act(lax.rem(me + k, devices))
            return carry

        if devices <= 64:
            for k in apart:
                step(k, 0)
        else:
            lax.fori_loop(1, devices, step, 0)

    barrier = pltpu.get_barrier_semaphore()
    each_other(
        lambda device: pl.semaphore_signal(
            barrier, inc=1, device_id=device, device_id_type=LOGICAL
        )
    )

    sent = []

    def start(src, dst, send, recv, device):
        pltpu.make_async_remote_copy(
            src_ref=src, dst_ref=dst, send_sem=send, recv_sem=recv,
            device_id=device, device_id_type=LOGICAL,
        ).start()

    def blocks(buf, amount, sem):
        span = buf.at[pl.ds(0, amount)]
        return pltpu.make_async_remote_copy(
            src_ref=span, dst_ref=span, send_sem=sem, recv_sem=sem,
            device_id=me, device_id_type=LOGICAL,
        )

    def to_line(src, buf, send, recv):
        for p in line_peers:
            start(src, buf.at[z], send, recv, p * plane + spot)
        sent.append(blocks(buf, line - 1, send))

    def to_plane(src, buf, send, recv):
        for p in plane_peers:
            start(src(p), buf.at[spot], send, recv, z * plane + p)
        sent.append(blocks(buf, plane - 1, send))

    def to_all(buf, send, recv):
        each_other(lambda device: start(buf.at[me], buf.at[me], send, recv, device))
        sent.append(blocks(buf, devices - 1, send))

    def arrived(buf, recv):
        blocks(buf, buf.shape[0] - 1, recv).wait_recv()

    lane = lax.broadcasted_iota(jnp.int32, (16, 128), 1)
    row_at = lax.broadcasted_iota(jnp.int32, (16, 128), 0)
    left16 = lane < 64

    def points_of(ref):
        scaled = rounded(ref[...].T * inv_ref[...])
        return jnp.concatenate([scaled[:32], scaled[32:]], axis=1).astype(BF16)

    def spread(columns):
        total = jnp.zeros((16, 128), F32)
        for q, one in enumerate(columns):
            total = jnp.where(lane == row_at + 16 * q, one, total)
        return jnp.sum(total, axis=0, keepdims=True)

    def gathered(ref, amount):
        total = jnp.sum(ref[...], axis=0)
        return [
            jnp.sum(jnp.where(lane == row_at + 16 * q, total, 0.0), axis=1, keepdims=True)
            for q in range(amount)
        ]

    def inner(wide, lane_blocks):
        total = jnp.zeros((16, 128), F32)
        for h, block in enumerate(lane_blocks):
            total += wide[:, 128 * h : 128 * h + 128] * block
        return jnp.sum(total, axis=1, keepdims=True)

    for load in loads[:3]:
        load.wait()
    target = target_ref[...]
    target2 = jnp.concatenate([target, target], axis=1)
    target_block = halves(target2)
    own_train = points_of(train_ref)
    lbuf[z, 0:32, :] = own_train
    lbuf[z, 32:48, :] = target_block
    pbuf[spot, 0:32, :] = own_train
    pbuf[spot, 32:48, :] = target_block
    pl.semaphore_wait(barrier, devices - 1)
    for p in line_peers:
        start(lbuf.at[z], lbuf.at[z], l_send, l_recv.at[z], p * plane + spot)
    sent.append(blocks(lbuf, line - 1, l_send))
    to_plane(lambda p: pbuf.at[spot], pbuf, p_send, p_recv)
    loads[3].wait()
    cbuf[spot] = points_of(cand_ref)
    to_plane(lambda p: cbuf.at[spot], cbuf, c_send, c_recv)
    loads[4].wait()
    noise = noise_ref[...]
    noise2 = jnp.concatenate([noise, noise], axis=1)

    def tile(slots, right, right_norm, high_ref, low_ref):
        left = jnp.concatenate([left_operand(lbuf[order[k], 0:32, :]) for k in slots], axis=0)
        matern_split(left, right, right_norm, high_ref, low_ref, 64 * slots[0])

    arrived(pbuf, p_recv)
    right_train, train_norm = right_operand([pbuf[s, 0:32, :] for s in range(plane)])
    tile([0], right_train, train_norm, train_hi, train_lo)
    for at in range(0, line, 4):
        slots = list(range(max(1, at), min(line, at + 4)))
        for k in slots:
            p = order[k]
            pltpu.make_async_remote_copy(
                src_ref=lbuf.at[p], dst_ref=lbuf.at[p], send_sem=l_send, recv_sem=l_recv.at[p],
                device_id=me, device_id_type=LOGICAL,
            ).wait_recv()
        tile(slots, right_train, train_norm, train_hi, train_lo)
    target_line = pairs([whole(lbuf[order[k], 32:48, :]) for k in range(line)])
    partial = applied(target_line, train_hi, train_lo)
    for s in range(plane):
        image_send[s] = packed(partial[:, 128 * (s // 2) : 128 * (s // 2) + 128], s % 2)
    to_plane(lambda p: image_send.at[p], image_buf, image_out, image_in)

    target_plane = pairs([whole(pbuf[s, 32:48, :]) for s in range(plane)])
    own_bb = jnp.sum(target * target, axis=1, keepdims=True)
    own_bnb = jnp.sum(noise * target * target, axis=1, keepdims=True)
    first_ref[me] = spread([inner(partial, target_plane) + own_bnb, own_bb])
    to_all(first_ref, first_send, first_recv)

    arrived(image_buf, image_in)
    image = image_send[spot]
    for p in plane_peers:
        image += image_buf[p]
    left8 = in_left(8)
    target_packed = jnp.where(left8, target2[0:8], target2[8:16])
    value = image + noise2 * target_packed
    vline[z] = value
    vplane[spot] = value
    to_line(vline.at[z], vline, vl_send, vl_recv)
    to_plane(lambda p: vplane.at[spot], vplane, vp_send, vp_recv)

    arrived(cbuf, c_recv)
    right_cand, cand_norm = right_operand([cbuf[s] for s in range(plane)])
    for at in range(0, line, 4):
        tile(list(range(at, min(line, at + 4))), right_cand, cand_norm, cand_hi, cand_lo)
    mean_b = applied(target_line, cand_hi, cand_lo)

    arrived(first_ref, first_recv)
    b_a_b, b_b = gathered(first_ref, 2)
    alpha = b_b / b_a_b

    def residuals(target_blocks, slots):
        return [
            block - alpha * values for block, values in zip(target_blocks, unpacked_pairs(slots))
        ]

    arrived(vline, vl_recv)
    residual_line = residuals(target_line, [vline[order[k]] for k in range(line)])
    image_r = applied(residual_line, train_hi, train_lo)
    mean_r = applied(residual_line, cand_hi, cand_lo)
    for s in range(plane):
        at = 128 * (s // 2)
        first, second = mean_b[:, at : at + 128], mean_r[:, at : at + 128]
        if s % 2:
            first = turned(first)
        else:
            second = turned(second)
        wsend[s] = jnp.where(left16, first, second)
    arrived(vplane, vp_recv)
    residual_plane = residuals(target_plane, [vplane[s] for s in range(plane)])
    value_own = unpacked(value, value)[:, 0:64]
    residual_own = target - alpha * value_own
    square = residual_own * residual_own
    own_rar = inner(image_r, residual_plane) + jnp.sum(noise * square, axis=1, keepdims=True)
    own_rr = jnp.sum(square, axis=1, keepdims=True)
    own_vr = jnp.sum(value_own * residual_own, axis=1, keepdims=True)
    last_ref[me] = spread([own_rar, own_rr, own_vr])
    to_all(last_ref, last_send, last_recv)
    to_plane(lambda p: wsend.at[p], wbuf, w_send, w_recv)

    arrived(wbuf, w_recv)
    means = wsend[spot]
    for p in plane_peers:
        means += wbuf[p]
    arrived(last_ref, last_recv)
    r_a_r, fresh, v_r = gathered(last_ref, 3)
    beta = fresh / b_b
    curve = r_a_r + 2.0 * beta * v_r + beta * beta * b_a_b
    alpha_two = fresh / curve
    share = alpha + alpha_two * beta
    out_ref[0:16, :] = share * target + alpha_two * residual_own
    out_ref[16:32, :] = share * means[:, 0:64] + alpha_two * means[:, 64:128]
    for copy in sent:
        copy.wait_send()


def per_device(rows, cols, train_points, cand_points, inv_length, noise, targets):
    vmem = pl.BlockSpec(memory_space=pltpu.VMEM)
    hbm = pl.BlockSpec(memory_space=pltpu.HBM)
    out = pltpu.VMEM((2 * targets.shape[0], targets.shape[1]), F32)
    operands = (
        train_points, cand_points, inv_length.reshape(1, -1), noise.reshape(1, -1), targets
    )
    dma = pltpu.SemaphoreType.DMA
    line, plane = rows // 2, 2 * cols
    kernel_tile = pltpu.VMEM((line * 64, plane * 64), BF16)
    both = pl.pallas_call(
        functools.partial(kernel, rows, cols),
        out_shape=out,
        in_specs=[hbm] * 5,
        out_specs=vmem,
        scratch_shapes=[pltpu.VMEM(operand.shape, F32) for operand in operands]
        + [
            pltpu.VMEM((line, 48, 128), BF16),
            pltpu.VMEM((plane, 48, 128), BF16),
            pltpu.VMEM((plane, 32, 128), BF16),
            kernel_tile, kernel_tile, kernel_tile, kernel_tile,
            pltpu.VMEM((plane, 8, 128), F32),
            pltpu.VMEM((plane, 8, 128), F32),
            pltpu.VMEM((line, 8, 128), F32),
            pltpu.VMEM((plane, 8, 128), F32),
            pltpu.VMEM((plane, 16, 128), F32),
            pltpu.VMEM((plane, 16, 128), F32),
            pltpu.VMEM((rows * cols, 1, 128), F32),
            pltpu.VMEM((rows * cols, 1, 128), F32),
            dma((5,)), dma((line,)),
        ]
        + [dma] * 17,
        compiler_params=pltpu.CompilerParams(
            collective_id=0, has_side_effects=True, vmem_limit_bytes=60 * 1024 * 1024
        ),
    )(*operands)
    return both[:16], both[16:]


def solution(mesh):
    placed = (
        P(None, ("row", "col")),
        P(None, ("row", "col")),
        P(),
        P(("row", "col")),
        P(None, ("row", "col")),
    )
    return jax.shard_map(
        functools.partial(per_device, mesh.shape["row"], mesh.shape["col"]),
        mesh=mesh,
        in_specs=placed,
        out_specs=(P(None, ("row", "col")), P(None, ("row", "col"))),
        check_vma=False,
    )
```

```python
import functools
import math

import jax
import jax.numpy as jnp
from jax import lax
from jax.experimental import pallas as pl
from jax.experimental.pallas import tpu as pltpu
from jax.sharding import PartitionSpec as P

LOGICAL = pl.DeviceIdType.LOGICAL
root_five = math.sqrt(5.0)
F32 = jnp.float32
BF16 = jnp.bfloat16


def in_left(rows):
    return lax.broadcasted_iota(jnp.int32, (rows, 128), 1) < 64


def turned(value):
    return pltpu.roll(value, 64, 1)


def rounded(value):
    return value.astype(BF16).astype(F32)


def halves(doubled):
    high = rounded(doubled)
    return jnp.where(in_left(doubled.shape[0]), high, doubled - high).astype(BF16)


def whole(block):
    value = block.astype(F32)
    return value + turned(value)


def packed(wide, second):
    top, bottom = wide[0:8], wide[8:16]
    if second:
        return jnp.where(in_left(8), turned(top), bottom)
    return jnp.where(in_left(8), top, turned(bottom))


def unpacked(first, second):
    left = in_left(8)
    return jnp.concatenate(
        [jnp.where(left, first, turned(second)), jnp.where(left, turned(first), second)], axis=0
    )


def both_halves(block):
    value = block.astype(F32)
    other = turned(value)
    return (value, other), (other, value)


def squares(value):
    square = value * value
    high = rounded(square)
    return high, square - high


def left_operand(block):
    left = in_left(block.shape[0])
    forms = []
    for here, there in both_halves(block):
        high, low = squares(there)[0], squares(here)[1]
        forms.append(
            jnp.concatenate([jnp.where(left, here, high), jnp.where(left, low, 0.0)], axis=1)
        )
    return jnp.concatenate(forms, axis=0).astype(BF16)


def right_operand(blocks):
    forms, square_forms = [], []
    for block in blocks:
        left = in_left(block.shape[0])
        for here, there in both_halves(block):
            forms.append(
                jnp.concatenate(
                    [jnp.where(left, -2.0 * here, 1.0), jnp.where(left, 1.0, 0.0)], axis=1
                )
            )
            square_forms.append(jnp.where(left, squares(here)[0], squares(there)[1]))
    operand = jnp.concatenate(forms, axis=0).astype(BF16)
    summed = lax.dot_general(
        jnp.ones((16, 128), BF16),
        jnp.concatenate(square_forms, axis=0).astype(BF16),
        (((1,), (1,)), ((), ())),
        preferred_element_type=F32,
    )
    return operand, summed[0:1]


def matern_split(left, right, right_norm, inner_ref, high_ref, low_ref, at):
    amount = left.shape[0]
    inner_ref[0:amount, :] = lax.dot_general(
        left, right, (((1,), (1,)), ((), ())), preferred_element_type=F32
    )

    def strip(index, carry):
        row = pl.multiple_of(index * 32, 32)
        dist = jnp.maximum(inner_ref[pl.ds(row, 32), :] + right_norm, 0.0)
        scaled = root_five * dist * lax.rsqrt(jnp.maximum(dist, 1e-30))
        kern = (1.0 + scaled + (5.0 / 3.0) * dist) * jnp.exp(-scaled)
        high = kern.astype(BF16)
        high_ref[pl.ds(at + row, 32), :] = high
        low_ref[pl.ds(at + row, 32), :] = (kern - high.astype(F32)).astype(BF16)
        return carry

    lax.fori_loop(0, amount // 32, strip, 0)


def pairs(slots):
    left = in_left(16)
    return [jnp.where(left, slots[2 * h], slots[2 * h + 1]) for h in range(len(slots) // 2)]


def unpacked_pairs(slots):
    return [unpacked(slots[2 * h], slots[2 * h + 1]) for h in range(len(slots) // 2)]


def applied(blocks, high_ref, low_ref):
    total = None
    for at in range(0, len(blocks), 2):
        wide = jnp.concatenate(blocks[at : at + 2], axis=1)
        high = rounded(wide)
        operand = jnp.concatenate([high, wide - high], axis=0).astype(BF16)
        span = slice(128 * at, 128 * at + wide.shape[1])
        part = jnp.dot(operand, high_ref[span, :], preferred_element_type=F32)
        part += jnp.dot(operand, low_ref[span, :], preferred_element_type=F32)
        total = part if total is None else total + part
    return total[:16] + total[16:]


def kernel(
    rows, cols,
    train_hbm, cand_hbm, inv_hbm, noise_hbm, target_hbm,
    out_ref,
    train_ref, cand_ref, inv_ref, noise_ref, target_ref,
    lbuf, pbuf, cbuf, inner_ref, train_hi, train_lo, cand_hi, cand_lo,
    image_send, image_buf, vline, vplane, wsend, wbuf, first_ref, last_ref,
    in_sem, l_recv,
    l_send, p_send, p_recv, c_send, c_recv, image_out, image_in,
    vl_send, vl_recv, vp_send, vp_recv, w_send, w_recv,
    first_send, first_recv, last_send, last_recv,
):
    loads = [
        pltpu.make_async_copy(src, dst, in_sem.at[n])
        for n, (src, dst) in enumerate(
            (
                (train_hbm, train_ref),
                (inv_hbm, inv_ref),
                (target_hbm, target_ref),
                (cand_hbm, cand_ref),
                (noise_hbm, noise_ref),
            )
        )
    ]
    for load in loads:
        load.start()
    a = lax.axis_index("row")
    b = lax.axis_index("col")
    devices = rows * cols
    line, plane = rows // 2, 2 * cols
    z = lax.div(a, 2)
    spot = lax.rem(a, 2) * cols + b
    me = z * plane + spot
    line_peers = [lax.rem(z + k, line) for k in range(1, line)]
    plane_peers = [lax.rem(spot + k, plane) for k in range(1, plane)]
    order = [z] + [lax.rem(z + line - k, line) for k in range(1, line)]

    def each_peer(mine, amount, act):
        def step(k, carry):
            act(lax.rem(mine + k, amount))
            return carry

        lax.fori_loop(1, amount, step, 0)

    def each_other(act):
        each_peer(me, devices, act)

    barrier = pltpu.get_barrier_semaphore()
    each_other(
        lambda device: pl.semaphore_signal(
            barrier, inc=1, device_id=device, device_id_type=LOGICAL
        )
    )

    sent = []

    def start(src, dst, send, recv, device):
        pltpu.make_async_remote_copy(
            src_ref=src, dst_ref=dst, send_sem=send, recv_sem=recv,
            device_id=device, device_id_type=LOGICAL,
        ).start()

    def blocks(buf, amount, sem):
        span = buf.at[pl.ds(0, amount)]
        return pltpu.make_async_remote_copy(
            src_ref=span, dst_ref=span, send_sem=sem, recv_sem=sem,
            device_id=me, device_id_type=LOGICAL,
        )

    def to_line(src, buf, send, recv):
        each_peer(z, line, lambda p: start(src, buf.at[z], send, recv, p * plane + spot))
        sent.append(blocks(buf, line - 1, send))

    def to_plane(src, buf, send, recv):
        each_peer(
            spot, plane, lambda p: start(src(p), buf.at[spot], send, recv, z * plane + p)
        )
        sent.append(blocks(buf, plane - 1, send))

    def to_all(buf, send, recv):
        each_other(lambda device: start(buf.at[me], buf.at[me], send, recv, device))
        sent.append(blocks(buf, devices - 1, send))

    def arrived(buf, recv):
        blocks(buf, buf.shape[0] - 1, recv).wait_recv()

    lane = lax.broadcasted_iota(jnp.int32, (16, 128), 1)
    row_at = lax.broadcasted_iota(jnp.int32, (16, 128), 0)
    left16 = lane < 64

    def points_of(ref):
        scaled = rounded(ref[...].T * inv_ref[...])
        return jnp.concatenate([scaled[:32], scaled[32:]], axis=1).astype(BF16)

    def spread(columns):
        total = jnp.zeros((16, 128), F32)
        for q, one in enumerate(columns):
            total = jnp.where(lane == row_at + 16 * q, one, total)
        return jnp.sum(total, axis=0, keepdims=True)

    def gathered(ref, amount):
        total = jnp.sum(ref[...], axis=0)
        return [
            jnp.sum(jnp.where(lane == row_at + 16 * q, total, 0.0), axis=1, keepdims=True)
            for q in range(amount)
        ]

    def inner(wide, lane_blocks):
        total = jnp.zeros((16, 128), F32)
        for h, block in enumerate(lane_blocks):
            total += wide[:, 128 * h : 128 * h + 128] * block
        return jnp.sum(total, axis=1, keepdims=True)

    for load in loads[:3]:
        load.wait()
    target = target_ref[...]
    target2 = jnp.concatenate([target, target], axis=1)
    target_block = halves(target2)
    own_train = points_of(train_ref)
    lbuf[z, 0:32, :] = own_train
    lbuf[z, 32:48, :] = target_block
    pbuf[spot, 0:32, :] = own_train
    pbuf[spot, 32:48, :] = target_block
    pl.semaphore_wait(barrier, devices - 1)
    to_line(lbuf.at[z], lbuf, l_send, l_recv.at[z])
    to_plane(lambda p: pbuf.at[spot], pbuf, p_send, p_recv)
    loads[3].wait()
    cbuf[spot] = points_of(cand_ref)
    to_plane(lambda p: cbuf.at[spot], cbuf, c_send, c_recv)
    loads[4].wait()
    noise = noise_ref[...]
    noise2 = jnp.concatenate([noise, noise], axis=1)

    def tile(slots, right, right_norm, high_ref, low_ref):
        left = jnp.concatenate([left_operand(lbuf[order[k], 0:32, :]) for k in slots], axis=0)
        matern_split(left, right, right_norm, inner_ref, high_ref, low_ref, 64 * slots[0])

    arrived(pbuf, p_recv)
    right_train, train_norm = right_operand([pbuf[s, 0:32, :] for s in range(plane)])
    tile([0], right_train, train_norm, train_hi, train_lo)
    for at in range(0, line, 4):
        slots = list(range(max(1, at), min(line, at + 4)))
        for k in slots:
            p = order[k]
            pltpu.make_async_remote_copy(
                src_ref=lbuf.at[p], dst_ref=lbuf.at[p], send_sem=l_send, recv_sem=l_recv.at[p],
                device_id=me, device_id_type=LOGICAL,
            ).wait_recv()
        tile(slots, right_train, train_norm, train_hi, train_lo)
    target_line = pairs([whole(lbuf[order[k], 32:48, :]) for k in range(line)])
    partial = applied(target_line, train_hi, train_lo)
    for s in range(plane):
        image_send[s] = packed(partial[:, 128 * (s // 2) : 128 * (s // 2) + 128], s % 2)
    to_plane(lambda p: image_send.at[p], image_buf, image_out, image_in)

    target_plane = pairs([whole(pbuf[s, 32:48, :]) for s in range(plane)])
    own_bb = jnp.sum(target * target, axis=1, keepdims=True)
    own_bnb = jnp.sum(noise * target * target, axis=1, keepdims=True)
    first_ref[me] = spread([inner(partial, target_plane) + own_bnb, own_bb])
    to_all(first_ref, first_send, first_recv)

    arrived(image_buf, image_in)
    image = image_send[spot]
    for p in plane_peers:
        image += image_buf[p]
    left8 = in_left(8)
    target_packed = jnp.where(left8, target2[0:8], target2[8:16])
    value = image + noise2 * target_packed
    vline[z] = value
    vplane[spot] = value
    to_line(vline.at[z], vline, vl_send, vl_recv)
    to_plane(lambda p: vplane.at[spot], vplane, vp_send, vp_recv)

    arrived(cbuf, c_recv)
    right_cand, cand_norm = right_operand([cbuf[s] for s in range(plane)])
    for at in range(0, line, 4):
        tile(list(range(at, min(line, at + 4))), right_cand, cand_norm, cand_hi, cand_lo)
    mean_b = applied(target_line, cand_hi, cand_lo)

    arrived(first_ref, first_recv)
    b_a_b, b_b = gathered(first_ref, 2)
    alpha = b_b / b_a_b

    def residuals(target_blocks, slots):
        return [
            block - alpha * values for block, values in zip(target_blocks, unpacked_pairs(slots))
        ]

    arrived(vline, vl_recv)
    residual_line = residuals(target_line, [vline[order[k]] for k in range(line)])
    image_r = applied(residual_line, train_hi, train_lo)
    mean_r = applied(residual_line, cand_hi, cand_lo)
    for s in range(plane):
        at = 128 * (s // 2)
        first, second = mean_b[:, at : at + 128], mean_r[:, at : at + 128]
        if s % 2:
            first = turned(first)
        else:
            second = turned(second)
        wsend[s] = jnp.where(left16, first, second)
    arrived(vplane, vp_recv)
    residual_plane = residuals(target_plane, [vplane[s] for s in range(plane)])
    value_own = unpacked(value, value)[:, 0:64]
    residual_own = target - alpha * value_own
    square = residual_own * residual_own
    own_rar = inner(image_r, residual_plane) + jnp.sum(noise * square, axis=1, keepdims=True)
    own_rr = jnp.sum(square, axis=1, keepdims=True)
    own_vr = jnp.sum(value_own * residual_own, axis=1, keepdims=True)
    last_ref[me] = spread([own_rar, own_rr, own_vr])
    to_all(last_ref, last_send, last_recv)
    to_plane(lambda p: wsend.at[p], wbuf, w_send, w_recv)

    arrived(wbuf, w_recv)
    means = wsend[spot]
    for p in plane_peers:
        means += wbuf[p]
    arrived(last_ref, last_recv)
    r_a_r, fresh, v_r = gathered(last_ref, 3)
    beta = fresh / b_b
    curve = r_a_r + 2.0 * beta * v_r + beta * beta * b_a_b
    alpha_two = fresh / curve
    share = alpha + alpha_two * beta
    out_ref[0:16, :] = share * target + alpha_two * residual_own
    out_ref[16:32, :] = share * means[:, 0:64] + alpha_two * means[:, 64:128]
    for copy in sent:
        copy.wait_send()


def per_device(rows, cols, train_points, cand_points, inv_length, noise, targets):
    vmem = pl.BlockSpec(memory_space=pltpu.VMEM)
    hbm = pl.BlockSpec(memory_space=pltpu.HBM)
    out = pltpu.VMEM((2 * targets.shape[0], targets.shape[1]), F32)
    operands = (
        train_points, cand_points, inv_length.reshape(1, -1), noise.reshape(1, -1), targets
    )
    dma = pltpu.SemaphoreType.DMA
    line, plane = rows // 2, 2 * cols
    kernel_tile = pltpu.VMEM((line * 64, plane * 64), BF16)
    both = pl.pallas_call(
        functools.partial(kernel, rows, cols),
        out_shape=out,
        in_specs=[hbm] * 5,
        out_specs=vmem,
        scratch_shapes=[pltpu.VMEM(operand.shape, F32) for operand in operands]
        + [
            pltpu.VMEM((line, 48, 128), BF16),
            pltpu.VMEM((plane, 48, 128), BF16),
            pltpu.VMEM((plane, 32, 128), BF16),
            pltpu.VMEM((64 * min(4, line), plane * 64), F32),
            kernel_tile, kernel_tile, kernel_tile, kernel_tile,
            pltpu.VMEM((plane, 8, 128), F32),
            pltpu.VMEM((plane, 8, 128), F32),
            pltpu.VMEM((line, 8, 128), F32),
            pltpu.VMEM((plane, 8, 128), F32),
            pltpu.VMEM((plane, 16, 128), F32),
            pltpu.VMEM((plane, 16, 128), F32),
            pltpu.VMEM((rows * cols, 1, 128), F32),
            pltpu.VMEM((rows * cols, 1, 128), F32),
            dma((5,)), dma((line,)),
        ]
        + [dma] * 17,
        compiler_params=pltpu.CompilerParams(
            collective_id=0, has_side_effects=True, vmem_limit_bytes=60 * 1024 * 1024
        ),
    )(*operands)
    return both[:16], both[16:]


def solution(mesh):
    placed = (
        P(None, ("row", "col")),
        P(None, ("row", "col")),
        P(),
        P(("row", "col")),
        P(None, ("row", "col")),
    )
    return jax.shard_map(
        functools.partial(per_device, mesh.shape["row"], mesh.shape["col"]),
        mesh=mesh,
        in_specs=placed,
        out_specs=(P(None, ("row", "col")), P(None, ("row", "col"))),
        check_vma=False,
    )
```

```python
import functools
import math

import jax
import jax.numpy as jnp
from jax import lax
from jax.experimental import pallas as pl
from jax.experimental.pallas import tpu as pltpu
from jax.sharding import PartitionSpec as P

LOGICAL = pl.DeviceIdType.LOGICAL
root_five = math.sqrt(5.0)
F32 = jnp.float32
BF16 = jnp.bfloat16


def in_left(rows):
    return lax.broadcasted_iota(jnp.int32, (rows, 128), 1) < 64


def turned(value):
    return pltpu.roll(value, 64, 1)


def rounded(value):
    return value.astype(BF16).astype(F32)


def halves(doubled):
    high = rounded(doubled)
    return jnp.where(in_left(doubled.shape[0]), high, doubled - high).astype(BF16)


def whole(block):
    value = block.astype(F32)
    return value + turned(value)


def packed(wide, second):
    top, bottom = wide[0:8], wide[8:16]
    if second:
        return jnp.where(in_left(8), turned(top), bottom)
    return jnp.where(in_left(8), top, turned(bottom))


def unpacked(first, second):
    left = in_left(8)
    return jnp.concatenate(
        [jnp.where(left, first, turned(second)), jnp.where(left, turned(first), second)], axis=0
    )


def both_halves(block):
    value = block.astype(F32)
    other = turned(value)
    return (value, other), (other, value)


def squares(value):
    square = value * value
    high = rounded(square)
    return high, square - high


def left_operand(block):
    left = in_left(block.shape[0])
    forms = []
    for here, there in both_halves(block):
        high, low = squares(there)[0], squares(here)[1]
        forms.append(
            jnp.concatenate([jnp.where(left, here, high), jnp.where(left, low, 0.0)], axis=1)
        )
    return jnp.concatenate(forms, axis=0).astype(BF16)


def right_operand(blocks):
    forms, square_forms = [], []
    for block in blocks:
        left = in_left(block.shape[0])
        for here, there in both_halves(block):
            forms.append(
                jnp.concatenate(
                    [jnp.where(left, -2.0 * here, 1.0), jnp.where(left, 1.0, 0.0)], axis=1
                )
            )
            square_forms.append(jnp.where(left, squares(here)[0], squares(there)[1]))
    operand = jnp.concatenate(forms, axis=0).astype(BF16)
    summed = lax.dot_general(
        jnp.ones((16, 128), BF16),
        jnp.concatenate(square_forms, axis=0).astype(BF16),
        (((1,), (1,)), ((), ())),
        preferred_element_type=F32,
    )
    return operand, summed[0:1]


def matern_split(left, right, right_norm, high_ref, low_ref, at):
    inner = lax.dot_general(
        left, right, (((1,), (1,)), ((), ())), preferred_element_type=F32
    )
    for row in range(0, inner.shape[0], 16):
        dist = jnp.maximum(inner[row : row + 16] + right_norm, 0.0)
        scaled = root_five * dist * lax.rsqrt(jnp.maximum(dist, 1e-30))
        kern = (1.0 + scaled + (5.0 / 3.0) * dist) * jnp.exp(-scaled)
        high = kern.astype(BF16)
        high_ref[at + row : at + row + 16, :] = high
        low_ref[at + row : at + row + 16, :] = (kern - high.astype(F32)).astype(BF16)


def pairs(slots):
    left = in_left(16)
    return [jnp.where(left, slots[2 * h], slots[2 * h + 1]) for h in range(len(slots) // 2)]


def unpacked_pairs(slots):
    return [unpacked(slots[2 * h], slots[2 * h + 1]) for h in range(len(slots) // 2)]


def applied(blocks, high_ref, low_ref):
    total = None
    for at in range(0, len(blocks), 2):
        wide = jnp.concatenate(blocks[at : at + 2], axis=1)
        high = rounded(wide)
        operand = jnp.concatenate([high, wide - high], axis=0).astype(BF16)
        span = slice(128 * at, 128 * at + wide.shape[1])
        part = jnp.dot(operand, high_ref[span, :], preferred_element_type=F32)
        part += jnp.dot(operand, low_ref[span, :], preferred_element_type=F32)
        total = part if total is None else total + part
    return total[:16] + total[16:]


def kernel(
    rows, cols,
    train_hbm, cand_hbm, inv_hbm, noise_hbm, target_hbm,
    out_ref,
    train_ref, cand_ref, inv_ref, noise_ref, target_ref,
    lbuf, pbuf, cbuf, train_hi, train_lo, cand_hi, cand_lo,
    image_send, image_buf, vline, vplane, wsend, wbuf, last_ref,
    in_sem, l_recv,
    l_send, p_send, p_recv, c_send, c_recv, image_out, image_in,
    vl_send, vl_recv, vp_send, vp_recv, w_send, w_recv,
    last_send, last_recv,
):
    loads = [
        pltpu.make_async_copy(src, dst, in_sem.at[n])
        for n, (src, dst) in enumerate(
            (
                (train_hbm, train_ref),
                (inv_hbm, inv_ref),
                (target_hbm, target_ref),
                (cand_hbm, cand_ref),
                (noise_hbm, noise_ref),
            )
        )
    ]
    for load in loads:
        load.start()
    a = lax.axis_index("row")
    b = lax.axis_index("col")
    devices = rows * cols
    line, plane = rows // 2, 2 * cols
    z = lax.div(a, 2)
    spot = lax.rem(a, 2) * cols + b
    me = z * plane + spot
    line_peers = [lax.rem(z + k, line) for k in range(1, line)]
    plane_peers = [lax.rem(spot + k, plane) for k in range(1, plane)]
    order = [z] + [lax.rem(z + line - k, line) for k in range(1, line)]

    apart = sorted(range(1, devices), key=lambda k: abs(k - devices // 2))

    def each_other(act):
        def step(k, carry):
            act(lax.rem(me + k, devices))
            return carry

        if devices <= 64:
            for k in apart:
                step(k, 0)
        else:
            lax.fori_loop(1, devices, step, 0)

    barrier = pltpu.get_barrier_semaphore()
    each_other(
        lambda device: pl.semaphore_signal(
            barrier, inc=1, device_id=device, device_id_type=LOGICAL
        )
    )

    sent = []

    def start(src, dst, send, recv, device):
        pltpu.make_async_remote_copy(
            src_ref=src, dst_ref=dst, send_sem=send, recv_sem=recv,
            device_id=device, device_id_type=LOGICAL,
        ).start()

    def blocks(buf, amount, sem):
        span = buf.at[pl.ds(0, amount)]
        return pltpu.make_async_remote_copy(
            src_ref=span, dst_ref=span, send_sem=sem, recv_sem=sem,
            device_id=me, device_id_type=LOGICAL,
        )

    def to_line(src, buf, send, recv):
        for p in line_peers:
            start(src, buf.at[z], send, recv, p * plane + spot)
        sent.append(blocks(buf, line - 1, send))

    def to_plane(src, buf, send, recv):
        for p in plane_peers:
            start(src(p), buf.at[spot], send, recv, z * plane + p)
        sent.append(blocks(buf, plane - 1, send))

    def to_all(buf, send, recv):
        each_other(lambda device: start(buf.at[me], buf.at[me], send, recv, device))
        sent.append(blocks(buf, devices - 1, send))

    def arrived(buf, recv):
        blocks(buf, buf.shape[0] - 1, recv).wait_recv()

    lane = lax.broadcasted_iota(jnp.int32, (16, 128), 1)
    row_at = lax.broadcasted_iota(jnp.int32, (16, 128), 0)
    left16 = lane < 64

    def points_of(ref):
        scaled = rounded(ref[...].T * inv_ref[...])
        return jnp.concatenate([scaled[:32], scaled[32:]], axis=1).astype(BF16)

    def spread(columns):
        total = jnp.zeros((16, 128), F32)
        for q, one in enumerate(columns):
            total = jnp.where(lane == row_at + 16 * q, one, total)
        return jnp.sum(total, axis=0, keepdims=True)

    def gathered(rows_in, amount):
        total = jnp.sum(rows_in, axis=0)
        return [
            jnp.sum(jnp.where(lane == row_at + 16 * q, total, 0.0), axis=1, keepdims=True)
            for q in range(amount)
        ]

    def inner(wide, lane_blocks):
        total = jnp.zeros((16, 128), F32)
        for h, block in enumerate(lane_blocks):
            total += wide[:, 128 * h : 128 * h + 128] * block
        return jnp.sum(total, axis=1, keepdims=True)

    for load in loads[:3]:
        load.wait()
    target = target_ref[...]
    target2 = jnp.concatenate([target, target], axis=1)
    target_block = halves(target2)
    own_train = points_of(train_ref)
    lbuf[z, 0:32, :] = own_train
    lbuf[z, 32:48, :] = target_block
    pbuf[spot, 0:32, :] = own_train
    pbuf[spot, 32:48, :] = target_block
    pl.semaphore_wait(barrier, devices - 1)
    for p in line_peers:
        start(lbuf.at[z], lbuf.at[z], l_send, l_recv.at[z], p * plane + spot)
    sent.append(blocks(lbuf, line - 1, l_send))
    to_plane(lambda p: pbuf.at[spot], pbuf, p_send, p_recv)
    loads[3].wait()
    cbuf[spot] = points_of(cand_ref)
    to_plane(lambda p: cbuf.at[spot], cbuf, c_send, c_recv)
    loads[4].wait()
    noise = noise_ref[...]
    noise2 = jnp.concatenate([noise, noise], axis=1)

    def tile(slots, right, right_norm, high_ref, low_ref):
        left = jnp.concatenate([left_operand(lbuf[order[k], 0:32, :]) for k in slots], axis=0)
        matern_split(left, right, right_norm, high_ref, low_ref, 64 * slots[0])

    arrived(pbuf, p_recv)
    right_train, train_norm = right_operand([pbuf[s, 0:32, :] for s in range(plane)])
    tile([0], right_train, train_norm, train_hi, train_lo)
    for at in range(0, line, 4):
        slots = list(range(max(1, at), min(line, at + 4)))
        for k in slots:
            p = order[k]
            pltpu.make_async_remote_copy(
                src_ref=lbuf.at[p], dst_ref=lbuf.at[p], send_sem=l_send, recv_sem=l_recv.at[p],
                device_id=me, device_id_type=LOGICAL,
            ).wait_recv()
        tile(slots, right_train, train_norm, train_hi, train_lo)
    target_line = pairs([whole(lbuf[order[k], 32:48, :]) for k in range(line)])
    partial = applied(target_line, train_hi, train_lo)
    target_plane = pairs([whole(pbuf[s, 32:48, :]) for s in range(plane)])
    own_bb = jnp.sum(target * target, axis=1, keepdims=True)
    own_bnb = jnp.sum(noise * target * target, axis=1, keepdims=True)
    first = spread([inner(partial, target_plane) + own_bnb, own_bb])
    first = jnp.broadcast_to(first, (8, 128))
    for s in range(plane):
        image_send[s, 0:8, :] = packed(partial[:, 128 * (s // 2) : 128 * (s // 2) + 128], s % 2)
        image_send[s, 8:16, :] = first
    to_plane(lambda p: image_send.at[p], image_buf, image_out, image_in)

    arrived(image_buf, image_in)
    image = image_send[spot]
    for p in plane_peers:
        image += image_buf[p]
    left8 = in_left(8)
    target_packed = jnp.where(left8, target2[0:8], target2[8:16])
    value = image[0:8] + noise2 * target_packed
    vline[z, 0:8, :] = value
    vline[z, 8:16, :] = image[8:16]
    vplane[spot] = value
    to_line(vline.at[z], vline, vl_send, vl_recv)
    to_plane(lambda p: vplane.at[spot], vplane, vp_send, vp_recv)

    arrived(cbuf, c_recv)
    right_cand, cand_norm = right_operand([cbuf[s] for s in range(plane)])
    for at in range(0, line, 4):
        tile(list(range(at, min(line, at + 4))), right_cand, cand_norm, cand_hi, cand_lo)
    mean_b = applied(target_line, cand_hi, cand_lo)

    arrived(vline, vl_recv)
    b_a_b, b_b = gathered(vline[:, 8:16, :][:, 0:1, :], 2)
    alpha = b_b / b_a_b

    def residuals(target_blocks, slots):
        return [
            block - alpha * values for block, values in zip(target_blocks, unpacked_pairs(slots))
        ]

    residual_line = residuals(target_line, [vline[order[k], 0:8, :] for k in range(line)])
    image_r = applied(residual_line, train_hi, train_lo)
    mean_r = applied(residual_line, cand_hi, cand_lo)
    for s in range(plane):
        at = 128 * (s // 2)
        first, second = mean_b[:, at : at + 128], mean_r[:, at : at + 128]
        if s % 2:
            first = turned(first)
        else:
            second = turned(second)
        wsend[s] = jnp.where(left16, first, second)
    arrived(vplane, vp_recv)
    residual_plane = residuals(target_plane, [vplane[s] for s in range(plane)])
    value_own = unpacked(value, value)[:, 0:64]
    residual_own = target - alpha * value_own
    square = residual_own * residual_own
    own_rar = inner(image_r, residual_plane) + jnp.sum(noise * square, axis=1, keepdims=True)
    own_rr = jnp.sum(square, axis=1, keepdims=True)
    own_vr = jnp.sum(value_own * residual_own, axis=1, keepdims=True)
    last_ref[me] = spread([own_rar, own_rr, own_vr])
    to_all(last_ref, last_send, last_recv)
    to_plane(lambda p: wsend.at[p], wbuf, w_send, w_recv)

    arrived(wbuf, w_recv)
    means = wsend[spot]
    for p in plane_peers:
        means += wbuf[p]
    arrived(last_ref, last_recv)
    r_a_r, fresh, v_r = gathered(last_ref[...], 3)
    beta = fresh / b_b
    curve = r_a_r + 2.0 * beta * v_r + beta * beta * b_a_b
    alpha_two = fresh / curve
    share = alpha + alpha_two * beta
    out_ref[0:16, :] = share * target + alpha_two * residual_own
    out_ref[16:32, :] = share * means[:, 0:64] + alpha_two * means[:, 64:128]
    for copy in sent:
        copy.wait_send()


def per_device(rows, cols, train_points, cand_points, inv_length, noise, targets):
    vmem = pl.BlockSpec(memory_space=pltpu.VMEM)
    hbm = pl.BlockSpec(memory_space=pltpu.HBM)
    out = pltpu.VMEM((2 * targets.shape[0], targets.shape[1]), F32)
    operands = (
        train_points, cand_points, inv_length.reshape(1, -1), noise.reshape(1, -1), targets
    )
    dma = pltpu.SemaphoreType.DMA
    line, plane = rows // 2, 2 * cols
    kernel_tile = pltpu.VMEM((line * 64, plane * 64), BF16)
    both = pl.pallas_call(
        functools.partial(kernel, rows, cols),
        out_shape=out,
        in_specs=[hbm] * 5,
        out_specs=vmem,
        scratch_shapes=[pltpu.VMEM(operand.shape, F32) for operand in operands]
        + [
            pltpu.VMEM((line, 48, 128), BF16),
            pltpu.VMEM((plane, 48, 128), BF16),
            pltpu.VMEM((plane, 32, 128), BF16),
            kernel_tile, kernel_tile, kernel_tile, kernel_tile,
            pltpu.VMEM((plane, 16, 128), F32),
            pltpu.VMEM((plane, 16, 128), F32),
            pltpu.VMEM((line, 16, 128), F32),
            pltpu.VMEM((plane, 8, 128), F32),
            pltpu.VMEM((plane, 16, 128), F32),
            pltpu.VMEM((plane, 16, 128), F32),
            pltpu.VMEM((rows * cols, 1, 128), F32),
            dma((5,)), dma((line,)),
        ]
        + [dma] * 15,
        compiler_params=pltpu.CompilerParams(
            collective_id=0, has_side_effects=True, vmem_limit_bytes=60 * 1024 * 1024
        ),
    )(*operands)
    return both[:16], both[16:]


def solution(mesh):
    placed = (
        P(None, ("row", "col")),
        P(None, ("row", "col")),
        P(),
        P(("row", "col")),
        P(None, ("row", "col")),
    )
    return jax.shard_map(
        functools.partial(per_device, mesh.shape["row"], mesh.shape["col"]),
        mesh=mesh,
        in_specs=placed,
        out_specs=(P(None, ("row", "col")), P(None, ("row", "col"))),
        check_vma=False,
    )
```

```python
import functools
import math

import jax
import jax.numpy as jnp
from jax import lax
from jax.experimental import pallas as pl
from jax.experimental.pallas import tpu as pltpu
from jax.sharding import PartitionSpec as P

MESH = pl.DeviceIdType.MESH
root_five = math.sqrt(5.0)
F32 = jnp.float32
BF16 = jnp.bfloat16


def in_left(rows):
    return lax.broadcasted_iota(jnp.int32, (rows, 128), 1) < 64


def turned(value):
    return pltpu.roll(value, 64, 1)


def rounded(value):
    return value.astype(BF16).astype(F32)


def halves(doubled):
    high = rounded(doubled)
    return jnp.where(in_left(doubled.shape[0]), high, doubled - high).astype(BF16)


def whole(block):
    value = block.astype(F32)
    return value + turned(value)


def packed(wide, second):
    top, bottom = wide[0:8], wide[8:16]
    if second:
        return jnp.where(in_left(8), turned(top), bottom)
    return jnp.where(in_left(8), top, turned(bottom))


def unpacked(first, second):
    left = in_left(8)
    return jnp.concatenate(
        [jnp.where(left, first, turned(second)), jnp.where(left, turned(first), second)], axis=0
    )


def both_halves(block):
    value = block.astype(F32)
    other = turned(value)
    return (value, other), (other, value)


def squares(value):
    square = value * value
    high = rounded(square)
    return high, square - high


def left_operand(block):
    left = in_left(block.shape[0])
    forms = []
    for here, there in both_halves(block):
        high, low = squares(there)[0], squares(here)[1]
        forms.append(
            jnp.concatenate([jnp.where(left, here, high), jnp.where(left, low, 0.0)], axis=1)
        )
    return jnp.concatenate(forms, axis=0).astype(BF16)


def right_operand(blocks):
    forms, square_forms = [], []
    for block in blocks:
        left = in_left(block.shape[0])
        for here, there in both_halves(block):
            forms.append(
                jnp.concatenate(
                    [jnp.where(left, -2.0 * here, 1.0), jnp.where(left, 1.0, 0.0)], axis=1
                )
            )
            square_forms.append(jnp.where(left, squares(here)[0], squares(there)[1]))
    operand = jnp.concatenate(forms, axis=0).astype(BF16)
    summed = lax.dot_general(
        jnp.ones((16, 128), BF16),
        jnp.concatenate(square_forms, axis=0).astype(BF16),
        (((1,), (1,)), ((), ())),
        preferred_element_type=F32,
    )
    return operand, summed[0:1]


def matern_split(left, right, right_norm, high_ref, low_ref, at):
    inner = lax.dot_general(
        left, right, (((1,), (1,)), ((), ())), preferred_element_type=F32
    )
    for row in range(0, inner.shape[0], 16):
        dist = jnp.maximum(inner[row : row + 16] + right_norm, 0.0)
        scaled = root_five * dist * lax.rsqrt(jnp.maximum(dist, 1e-30))
        kern = (1.0 + scaled + (5.0 / 3.0) * dist) * jnp.exp(-scaled)
        high = kern.astype(BF16)
        high_ref[at + row : at + row + 16, :] = high
        low_ref[at + row : at + row + 16, :] = (kern - high.astype(F32)).astype(BF16)


def pairs(slots):
    left = in_left(16)
    return [jnp.where(left, slots[2 * h], slots[2 * h + 1]) for h in range(len(slots) // 2)]


def unpacked_pairs(slots):
    return [unpacked(slots[2 * h], slots[2 * h + 1]) for h in range(len(slots) // 2)]


def applied(blocks, high_ref, low_ref):
    total = None
    for at in range(0, len(blocks), 2):
        wide = jnp.concatenate(blocks[at : at + 2], axis=1)
        high = rounded(wide)
        operand = jnp.concatenate([high, wide - high], axis=0).astype(BF16)
        span = slice(128 * at, 128 * at + wide.shape[1])
        part = jnp.dot(operand, high_ref[span, :], preferred_element_type=F32)
        part += jnp.dot(operand, low_ref[span, :], preferred_element_type=F32)
        total = part if total is None else total + part
    return total[:16] + total[16:]


def kernel(
    rows, cols,
    train_hbm, cand_hbm, inv_hbm, noise_hbm, target_hbm,
    out_ref,
    train_ref, cand_ref, inv_ref, noise_ref, target_ref,
    lbuf, pbuf, cbuf, train_hi, train_lo, cand_hi, cand_lo,
    image_send, image_buf, vline, vplane, wsend, wbuf, first_ref, last_ref,
    in_sem, l_recv,
    l_send, p_send, p_recv, c_send, c_recv, image_out, image_in,
    vl_send, vl_recv, vp_send, vp_recv, w_send, w_recv,
    first_send, first_recv, last_send, last_recv,
):
    loads = [
        pltpu.make_async_copy(src, dst, in_sem.at[n])
        for n, (src, dst) in enumerate(
            (
                (train_hbm, train_ref),
                (inv_hbm, inv_ref),
                (target_hbm, target_ref),
                (cand_hbm, cand_ref),
                (noise_hbm, noise_ref),
            )
        )
    ]
    for load in loads:
        load.start()
    a = lax.axis_index("row")
    b = lax.axis_index("col")
    devices = rows * cols
    me = a * cols + b
    z, core = lax.div(a, 2), lax.rem(a, 2)
    line, plane = rows // 2, 2 * cols
    spot = core * cols + b
    line_peers = [lax.rem(z + k, line) for k in range(1, line)]
    plane_peers = [lax.rem(spot + k, plane) for k in range(1, plane)]
    order = [z] + [lax.rem(z + line - k, line) for k in range(1, line)]

    def each_other(act):
        def step(k, carry):
            other = lax.rem(me + k, devices)
            act((lax.div(other, cols), lax.rem(other, cols)))
            return carry

        if devices <= 64:
            for k in range(1, devices):
                step(k, 0)
        else:
            lax.fori_loop(1, devices, step, 0)

    barrier = pltpu.get_barrier_semaphore()
    each_other(
        lambda device: pl.semaphore_signal(
            barrier, inc=1, device_id=device, device_id_type=MESH
        )
    )

    sent = []

    def start(src, dst, send, recv, device):
        pltpu.make_async_remote_copy(
            src_ref=src, dst_ref=dst, send_sem=send, recv_sem=recv,
            device_id=device, device_id_type=MESH,
        ).start()

    def blocks(buf, amount, sem):
        span = buf.at[pl.ds(0, amount)]
        return pltpu.make_async_remote_copy(
            src_ref=span, dst_ref=span, send_sem=sem, recv_sem=sem,
            device_id=(a, b), device_id_type=MESH,
        )

    def to_line(src, buf, send, recv):
        for p in line_peers:
            start(src, buf.at[z], send, recv, (2 * p + core, b))
        sent.append(blocks(buf, line - 1, send))

    def to_plane(src, buf, send, recv):
        for p in plane_peers:
            device = (2 * z + lax.div(p, cols), lax.rem(p, cols))
            start(src(p), buf.at[spot], send, recv, device)
        sent.append(blocks(buf, plane - 1, send))

    def to_all(buf, send, recv):
        each_other(lambda device: start(buf.at[me], buf.at[me], send, recv, device))
        sent.append(blocks(buf, devices - 1, send))

    def arrived(buf, recv):
        blocks(buf, buf.shape[0] - 1, recv).wait_recv()

    lane = lax.broadcasted_iota(jnp.int32, (16, 128), 1)
    row_at = lax.broadcasted_iota(jnp.int32, (16, 128), 0)
    left16 = lane < 64

    def points_of(ref):
        scaled = rounded(ref[...].T * inv_ref[...])
        return jnp.concatenate([scaled[:32], scaled[32:]], axis=1).astype(BF16)

    def spread(columns):
        total = jnp.zeros((16, 128), F32)
        for q, one in enumerate(columns):
            total = jnp.where(lane == row_at + 16 * q, one, total)
        return jnp.sum(total, axis=0, keepdims=True)

    def gathered(ref, amount):
        total = jnp.sum(ref[...], axis=0)
        return [
            jnp.sum(jnp.where(lane == row_at + 16 * q, total, 0.0), axis=1, keepdims=True)
            for q in range(amount)
        ]

    def inner(wide, lane_blocks):
        total = jnp.zeros((16, 128), F32)
        for h, block in enumerate(lane_blocks):
            total += wide[:, 128 * h : 128 * h + 128] * block
        return jnp.sum(total, axis=1, keepdims=True)

    for load in loads[:3]:
        load.wait()
    target = target_ref[...]
    target2 = jnp.concatenate([target, target], axis=1)
    target_block = halves(target2)
    own_train = points_of(train_ref)
    lbuf[z, 0:32, :] = own_train
    lbuf[z, 32:48, :] = target_block
    pbuf[spot, 0:32, :] = own_train
    pbuf[spot, 32:48, :] = target_block
    pl.semaphore_wait(barrier, devices - 1)
    for p in line_peers:
        start(lbuf.at[z], lbuf.at[z], l_send, l_recv.at[z], (2 * p + core, b))
    sent.append(blocks(lbuf, line - 1, l_send))
    to_plane(lambda p: pbuf.at[spot], pbuf, p_send, p_recv)
    loads[3].wait()
    cbuf[spot] = points_of(cand_ref)
    to_plane(lambda p: cbuf.at[spot], cbuf, c_send, c_recv)
    loads[4].wait()
    noise = noise_ref[...]
    noise2 = jnp.concatenate([noise, noise], axis=1)

    def tile(slots, right, right_norm, high_ref, low_ref):
        left = jnp.concatenate([left_operand(lbuf[order[k], 0:32, :]) for k in slots], axis=0)
        matern_split(left, right, right_norm, high_ref, low_ref, 64 * slots[0])

    arrived(pbuf, p_recv)
    right_train, train_norm = right_operand([pbuf[s, 0:32, :] for s in range(plane)])
    tile([0], right_train, train_norm, train_hi, train_lo)
    for at in range(0, line, 4):
        slots = list(range(max(1, at), min(line, at + 4)))
        for k in slots:
            p = order[k]
            pltpu.make_async_remote_copy(
                src_ref=lbuf.at[p], dst_ref=lbuf.at[p], send_sem=l_send, recv_sem=l_recv.at[p],
                device_id=(a, b), device_id_type=MESH,
            ).wait_recv()
        tile(slots, right_train, train_norm, train_hi, train_lo)
    target_line = pairs([whole(lbuf[order[k], 32:48, :]) for k in range(line)])
    partial = applied(target_line, train_hi, train_lo)
    for s in range(plane):
        image_send[s] = packed(partial[:, 128 * (s // 2) : 128 * (s // 2) + 128], s % 2)
    to_plane(lambda p: image_send.at[p], image_buf, image_out, image_in)

    target_plane = pairs([whole(pbuf[s, 32:48, :]) for s in range(plane)])
    own_bb = jnp.sum(target * target, axis=1, keepdims=True)
    own_bnb = jnp.sum(noise * target * target, axis=1, keepdims=True)

    arrived(cbuf, c_recv)
    right_cand, cand_norm = right_operand([cbuf[s] for s in range(plane)])
    for at in range(0, line, 4):
        tile(list(range(at, min(line, at + 4))), right_cand, cand_norm, cand_hi, cand_lo)

    arrived(image_buf, image_in)
    image = image_send[spot]
    for p in plane_peers:
        image += image_buf[p]
    left8 = in_left(8)
    target_packed = jnp.where(left8, target2[0:8], target2[8:16])
    value = image + noise2 * target_packed
    vline[z] = value
    vplane[spot] = value
    to_line(vline.at[z], vline, vl_send, vl_recv)
    to_plane(lambda p: vplane.at[spot], vplane, vp_send, vp_recv)

    first_ref[me] = spread([inner(partial, target_plane) + own_bnb, own_bb])
    to_all(first_ref, first_send, first_recv)
    mean_b = applied(target_line, cand_hi, cand_lo)

    arrived(first_ref, first_recv)
    b_a_b, b_b = gathered(first_ref, 2)
    alpha = b_b / b_a_b

    def residuals(target_blocks, slots):
        return [
            block - alpha * values for block, values in zip(target_blocks, unpacked_pairs(slots))
        ]

    arrived(vline, vl_recv)
    residual_line = residuals(target_line, [vline[order[k]] for k in range(line)])
    image_r = applied(residual_line, train_hi, train_lo)
    mean_r = applied(residual_line, cand_hi, cand_lo)
    for s in range(plane):
        at = 128 * (s // 2)
        first, second = mean_b[:, at : at + 128], mean_r[:, at : at + 128]
        if s % 2:
            first = turned(first)
        else:
            second = turned(second)
        wsend[s] = jnp.where(left16, first, second)
    arrived(vplane, vp_recv)
    residual_plane = residuals(target_plane, [vplane[s] for s in range(plane)])
    value_own = unpacked(value, value)[:, 0:64]
    residual_own = target - alpha * value_own
    square = residual_own * residual_own
    own_rar = inner(image_r, residual_plane) + jnp.sum(noise * square, axis=1, keepdims=True)
    own_rr = jnp.sum(square, axis=1, keepdims=True)
    own_vr = jnp.sum(value_own * residual_own, axis=1, keepdims=True)
    last_ref[me] = spread([own_rar, own_rr, own_vr])
    to_plane(lambda p: wsend.at[p], wbuf, w_send, w_recv)
    to_all(last_ref, last_send, last_recv)

    arrived(wbuf, w_recv)
    means = wsend[spot]
    for p in plane_peers:
        means += wbuf[p]
    arrived(last_ref, last_recv)
    r_a_r, fresh, v_r = gathered(last_ref, 3)
    beta = fresh / b_b
    curve = r_a_r + 2.0 * beta * v_r + beta * beta * b_a_b
    alpha_two = fresh / curve
    share = alpha + alpha_two * beta
    out_ref[0:16, :] = share * target + alpha_two * residual_own
    out_ref[16:32, :] = share * means[:, 0:64] + alpha_two * means[:, 64:128]
    for copy in sent:
        copy.wait_send()


def per_device(rows, cols, train_points, cand_points, inv_length, noise, targets):
    vmem = pl.BlockSpec(memory_space=pltpu.VMEM)
    hbm = pl.BlockSpec(memory_space=pltpu.HBM)
    out = pltpu.VMEM((2 * targets.shape[0], targets.shape[1]), F32)
    operands = (
        train_points, cand_points, inv_length.reshape(1, -1), noise.reshape(1, -1), targets
    )
    dma = pltpu.SemaphoreType.DMA
    line, plane = rows // 2, 2 * cols
    kernel_tile = pltpu.VMEM((line * 64, plane * 64), BF16)
    both = pl.pallas_call(
        functools.partial(kernel, rows, cols),
        out_shape=out,
        in_specs=[hbm] * 5,
        out_specs=vmem,
        scratch_shapes=[pltpu.VMEM(operand.shape, F32) for operand in operands]
        + [
            pltpu.VMEM((line, 48, 128), BF16),
            pltpu.VMEM((plane, 48, 128), BF16),
            pltpu.VMEM((plane, 32, 128), BF16),
            kernel_tile, kernel_tile, kernel_tile, kernel_tile,
            pltpu.VMEM((plane, 8, 128), F32),
            pltpu.VMEM((plane, 8, 128), F32),
            pltpu.VMEM((line, 8, 128), F32),
            pltpu.VMEM((plane, 8, 128), F32),
            pltpu.VMEM((plane, 16, 128), F32),
            pltpu.VMEM((plane, 16, 128), F32),
            pltpu.VMEM((rows * cols, 1, 128), F32),
            pltpu.VMEM((rows * cols, 1, 128), F32),
            dma((5,)), dma((line,)),
        ]
        + [dma] * 17,
        compiler_params=pltpu.CompilerParams(
            collective_id=0, has_side_effects=True, vmem_limit_bytes=60 * 1024 * 1024
        ),
    )(*operands)
    return both[:16], both[16:]


def solution(mesh):
    placed = (
        P(None, ("row", "col")),
        P(None, ("row", "col")),
        P(),
        P(("row", "col")),
        P(None, ("row", "col")),
    )
    return jax.shard_map(
        functools.partial(per_device, mesh.shape["row"], mesh.shape["col"]),
        mesh=mesh,
        in_specs=placed,
        out_specs=(P(None, ("row", "col")), P(None, ("row", "col"))),
        check_vma=False,
    )
```
